32 devices in a mesh: dp: 16 (over z, y, core), fsdp: 2 (over x).
Axes of the slice: x: 2, y: 2, z: 4, core: 2. Of those that a mesh axis runs over, the one named last changes fastest.
Arguments:
- context: bfloat16 [8192, 2048], P(('dp', 'fsdp')), may hold values from -6 to 6
- residual: bfloat16 [8192, 2048], P(('dp', 'fsdp')), may hold values from -6 to 6
- weight: bfloat16 [2048, 2048], P('fsdp'), may hold values from -0.125 to 0.125
- gain: bfloat16 [2048], replicated, may hold values from 0.099609375 to 1.8984375
- pattern: int32 [32, 16], P(('dp', 'fsdp')), may hold values from 0 to 1, as said below
- positive: int32 [64], P(('dp', 'fsdp')), may hold values from 0 to 1
Outputs:
- losses: float32 [64], P(('dp', 'fsdp'))
- grad_weight: float32 [2048, 2048], P('fsdp', 'dp')
The draws below stay inside these ranges and needn't reach their ends.
Inputs may be any that keep to these rules, and one draw needn't show every extreme that they name: pattern is 0 or 1; row b always holds 1 at column b // 2 (its own block); rows hold different numbers of ones.
All inputs are finite; a program needn't handle non-finite values.
Results may differ from the reference program's by a relative error of at most 0.0046.
Values may be sent and summed in bfloat16 or wider, within the bound.
A program may use at most 64 MiB of HBM per device.

```python
import jax
import jax.numpy as jnp
from jax import lax

DM = 2048
HD = 2048
LEN = 64
SEQ_DEV = 2
BLOCKS = 32
POOL_BLOCKS = 16
QUERIES = 64
TOKENS = 8192
N_DP = 16
N_FSDP = 2


def draw_pattern(key, part):
    first_key, second_key = jax.random.split(jax.random.fold_in(key, 11))
    limits = jax.random.randint(first_key, (BLOCKS, 1), 1, POOL_BLOCKS + 1)
    values = jax.random.randint(second_key, (BLOCKS, POOL_BLOCKS), 0, POOL_BLOCKS)
    owners = jnp.arange(BLOCKS, dtype=jnp.int32)[:, None] // (BLOCKS // POOL_BLOCKS)
    itself = owners == jnp.arange(POOL_BLOCKS, dtype=jnp.int32)[None, :]
    return jnp.logical_or(values < limits, itself).astype(jnp.int32)


def touch_ends(array, own_key, smallest, top_value):
    spot = [jax.random.randint(jax.random.fold_in(own_key, axis), (), 0, length) for axis, length in enumerate(array.shape)]
    main_axis = array.shape.index(max(array.shape))
    neighbour = spot[:main_axis] + [(spot[main_axis] + 1) % array.shape[main_axis]] + spot[main_axis + 1:]
    return array.at[tuple(spot)].set(smallest).at[tuple(neighbour)].set(top_value)


def block_levels(stream_key, dims, cuts, least, largest):
    level = 1.0
    for dim, shards_of in cuts:
        steps = jax.random.uniform(jax.random.fold_in(jax.random.fold_in(stream_key, 6), dim), (shards_of,), jnp.float32, least / len(cuts), largest / len(cuts))
        level = level * jnp.repeat(jnp.exp(steps), dims[dim] // shards_of).reshape((-1,) + (1,) * (len(dims) - 1 - dim))
    return level


def gaussian(key, extent, deviation, bound, cuts=(), kind=jnp.bfloat16):
    drawn = deviation * jax.random.normal(key, extent, jnp.float32)
    if cuts:
        drawn = drawn * block_levels(key, extent, cuts, -0.22, 0.18)
    return jnp.clip(drawn, -bound, bound).astype(kind)


def setup_inputs(seed: int = 0) -> dict:
    splits = jax.random.split(jax.random.key(seed), 7)
    context = gaussian(splits[0], (TOKENS, HD), 1.0, 6.0, ((0, 32),))
    residual = gaussian(splits[1], (TOKENS, DM), 1.0, 6.0, ((0, 32),))
    weight = gaussian(splits[2], (HD, DM), HD ** -0.5, 0.125, ((0, 2),))
    gain = jnp.clip(1.0 + 0.18 * jax.random.normal(splits[3], (DM,), jnp.float32), 0.099609375, 1.8984375).astype(jnp.bfloat16)
    pattern = draw_pattern(jax.random.fold_in(splits[6], 71), 0)
    positive = touch_ends(jax.random.randint(splits[5], (QUERIES,), 0, SEQ_DEV), jax.random.fold_in(splits[5], 1), 0, SEQ_DEV - 1).astype(jnp.int32)
    return {"context": context, "residual": residual, "weight": weight, "gain": gain, "pattern": pattern, "positive": positive}


def forward_block(context_rows, residual_rows, weight, gain):
    projected = jnp.dot(context_rows, weight, preferred_element_type=jnp.float32)
    hidden = residual_rows.astype(jnp.float32) + projected
    inv = lax.rsqrt(lax.optimization_barrier(jnp.mean(hidden * hidden, axis=1, keepdims=True)) + 1e-05)
    normed = hidden * inv * gain.astype(jnp.float32)
    pooled = normed.reshape(2 * SEQ_DEV, LEN, DM).mean(axis=1)
    scale = lax.rsqrt(lax.optimization_barrier(jnp.sum(pooled * pooled, axis=1, keepdims=True)) + 1e-06)
    unit = pooled * scale
    return (hidden, inv, scale, unit)

def backward_block(hidden, inv, scale, unit, d_embed, gain):
    d_pooled = (d_embed - unit * lax.optimization_barrier(jnp.sum(unit * d_embed, axis=1, keepdims=True))) * scale
    d_normed = jnp.broadcast_to(d_pooled[:, None, :] / LEN, (2 * SEQ_DEV, LEN, DM)).reshape(2 * SEQ_DEV * LEN, DM)
    gated = d_normed * gain.astype(jnp.float32)
    d_hidden = inv * gated - hidden * inv * inv * inv * lax.optimization_barrier(jnp.mean(hidden * gated, axis=1, keepdims=True))
    return d_hidden.astype(jnp.bfloat16)

def reference(context, residual, weight, gain, pattern, positive):
    blocks = N_DP * N_FSDP
    rows = 2 * SEQ_DEV * LEN
    context_blocks = context.reshape(blocks, rows, HD)
    residual_blocks = residual.reshape(blocks, rows, DM)

    def embed_block(item):
        return forward_block(item[0], item[1], weight, gain)[3].astype(jnp.bfloat16)
    embed = lax.map(embed_block, (context_blocks, residual_blocks))
    query = embed[:, :SEQ_DEV].reshape(N_DP, N_FSDP, SEQ_DEV, DM).astype(jnp.float32)
    premise = embed[:, SEQ_DEV:].reshape(N_DP, N_FSDP, SEQ_DEV, DM)
    pool = jnp.transpose(premise, (1, 0, 2, 3)).reshape(N_FSDP, N_DP * SEQ_DEV, DM).astype(jnp.float32)
    scores = 20.0 * jnp.einsum('dfsk,fpk->dfsp', query, pool)
    allowed = jnp.repeat(pattern.reshape(N_DP, N_FSDP, N_DP), SEQ_DEV, axis=2)[:, :, None, :].astype(jnp.float32)
    target = (jnp.arange(N_DP, dtype=jnp.int32)[:, None, None] * SEQ_DEV + positive.reshape(N_DP, N_FSDP, SEQ_DEV)).astype(jnp.int32)
    columns = jnp.arange(N_DP * SEQ_DEV, dtype=jnp.int32)
    onehot = (columns[None, None, None, :] == target[..., None]).astype(jnp.float32)
    weighted = allowed * jnp.exp(scores)
    total = lax.optimization_barrier(jnp.sum(weighted, axis=3, keepdims=True))
    losses = jnp.log(total[..., 0]) - lax.optimization_barrier(jnp.sum(onehot * scores, axis=3))
    coeff = (weighted / total - onehot).astype(jnp.bfloat16).astype(jnp.float32)
    d_query = 20.0 * jnp.einsum('dfsp,fpk->dfsk', coeff, pool)
    d_pool = 20.0 * jnp.einsum('dfsp,dfsk->fpk', coeff, query)
    d_premise = jnp.transpose(d_pool.reshape(N_FSDP, N_DP, SEQ_DEV, DM), (1, 0, 2, 3))
    d_embed = jnp.concatenate([d_query, d_premise], axis=2).reshape(blocks, 2 * SEQ_DEV, DM)

    def accumulate(grad, item):
        context_rows, residual_rows, d_rows = item
        hidden, inv, scale, unit = forward_block(context_rows, residual_rows, weight, gain)
        d_hidden = backward_block(hidden, inv, scale, unit, d_rows, gain)
        term = lax.dot_general(context_rows, d_hidden, (((0,), (0,)), ((), ())), preferred_element_type=jnp.float32)
        return (grad + term, None)
    grad_weight, unused = lax.scan(accumulate, jnp.zeros((HD, DM), jnp.float32), (context_blocks, residual_blocks, d_embed))
    return (losses.reshape(-1), grad_weight)
```

```python
import functools

import jax
import jax.numpy as jnp
import numpy as np
from jax import lax
from jax.experimental import pallas as pl
from jax.experimental.pallas import tpu as pltpu
from jax.sharding import PartitionSpec as P

MESH = pl.DeviceIdType.MESH
F32 = jnp.float32
BF16 = jnp.bfloat16
HIGH = lax.Precision.HIGHEST
NT = (((1,), (1,)), ((), ()))


def flip(index, mask):
    out = index
    bit = 1
    while bit <= mask:
        if mask & bit:
            out = out + bit * (1 - 2 * lax.rem(lax.div(index, bit), 2))
        bit *= 2
    return out


def count_copies(nd, nf):
    nz = nd // 4
    return (nf - 1) * 16 + (nf - 1) + nf + (nd - 1) + (2 * nf - 1) * nz + nz + nz - 1


def kernel(
    nd,
    nf,
    seqs,
    context_hbm,
    residual_hbm,
    weight_hbm,
    gain_ref,
    pattern_ref,
    positive_ref,
    spread_ref,
    select_ref,
    same_ref,
    rows_ref,
    loss_ref,
    grad_ref,
    ctx,
    res,
    wg,
    hid,
    invs,
    ctx_t,
    ctx_all,
    msg,
    pool,
    dhs,
    dh_all,
    y_send,
    y_recv,
    kept,
    z_send,
    z_recv,
    local_sem,
    send_sem,
    recv_sem,
):
    d = lax.axis_index("dp")
    f = lax.axis_index("fsdp")
    tokens, width = ctx.shape
    nz = nd // 4
    bw = width // nd
    core = lax.rem(d, 2)
    y = lax.rem(lax.div(d, 2), 2)
    z = lax.div(d, 4)
    spot = lax.rem(d, 8)
    depth = wg.shape[1] * wg.shape[2] * wg.shape[3]
    length = tokens // (2 * seqs)
    other = lambda k: lax.rem(f + k, nf)
    source = lambda k: lax.rem(f + nf - k, nf)

    started = []

    def send(src, dst, dd, ff):
        slot = len(started)
        copy = pltpu.make_async_remote_copy(
            src_ref=src,
            dst_ref=dst,
            send_sem=send_sem.at[slot],
            recv_sem=recv_sem.at[slot],
            device_id=(dd, ff),
            device_id_type=MESH,
        )
        copy.start()
        started.append(copy)
        return copy

    own = pltpu.make_async_copy(weight_hbm, wg.at[f], local_sem.at[0])
    own.start()
    load_ctx = pltpu.make_async_copy(context_hbm, ctx, local_sem.at[1])
    load_ctx.start()
    load_res = pltpu.make_async_copy(residual_hbm, res, local_sem.at[2])
    load_res.start()

    barrier = pltpu.get_barrier_semaphore()
    partners = [(lax.rem(d + s, nd), f) for s in range(1, nd)]
    partners += [(d, other(k)) for k in range(1, nf)]
    partners += [(flip(d, 1), other(k)) for k in range(1, nf)]
    for partner in partners:
        pl.semaphore_signal(barrier, inc=1, device_id=partner, device_id_type=MESH)
    pl.semaphore_wait(barrier, len(partners))

    direct = {}
    for h in range(2):
        for k in range(1, nf):
            direct[h, k] = send(weight_hbm.at[spot, h], wg.at[f, spot, h], d, other(k))

    def pass_on(k, place, h, mask):
        ref = wg.at[source(k), place, h]
        return send(ref, ref, flip(d, mask), f)

    load_ctx.wait()
    for part in range(nf):
        ctx_t[part] = ctx[:, part * depth : (part + 1) * depth].T
    ctx_all[core, f] = ctx_t[f]
    own.wait()
    load_res.wait()

    tile = 256

    def project(shard, first):
        def step(n, carry):
            cols = pl.ds(pl.multiple_of(n * tile, tile), tile)
            left = ctx[:, pl.ds(pl.multiple_of(shard * depth, 128), depth)]
            right = wg[shard, :, :, :, cols].reshape(depth, tile)
            before = res[:, cols].astype(F32) if first else hid[:, cols]
            hid[:, cols] = before + jnp.dot(left, right, preferred_element_type=F32)
            return carry

        lax.fori_loop(0, width // tile, step, 0)

    project(f, True)

    from_y, from_z, from_core = {}, {}, []
    for h in range(2):
        for k in range(1, nf):
            direct[h, k].wait_recv()
            from_y[h, k] = pass_on(k, spot, h, 2)
            from_z[h, k] = pass_on(k, spot, h, 4)
            from_core.append(pass_on(k, spot, h, 1))
    near_y, near_z, far = flip(spot, 2), flip(spot, 4), flip(spot, 6)
    ctx_copies = [
        send(ctx_t.at[other(k)], ctx_all.at[core, f], d, other(k)) for k in range(1, nf)
    ]
    sibling_ctx = [send(ctx_all.at[core, f], ctx_all.at[core, f], flip(d, 1), f)]
    across_y, across_z = {}, {}
    for k in range(1, nf):
        from_z[0, k].wait_recv()
        across_y[k] = pass_on(k, near_z, 0, 2)
        from_core.append(pass_on(k, near_z, 0, 1))
    for k in range(1, nf):
        from_y[0, k].wait_recv()
        from_core.append(pass_on(k, near_y, 0, 1))
    for k in range(1, nf):
        from_y[1, k].wait_recv()
        across_z[k] = pass_on(k, near_y, 1, 4)
        from_core.append(pass_on(k, near_y, 1, 1))
    for k in range(1, nf):
        from_z[1, k].wait_recv()
        from_core.append(pass_on(k, near_z, 1, 1))
    for k in range(1, nf):
        across_y[k].wait_recv()
        from_core.append(pass_on(k, far, 0, 1))
    for k in range(1, nf):
        across_z[k].wait_recv()
        from_core.append(pass_on(k, far, 1, 1))
    for copy in from_core:
        copy.wait_recv()
    for k in range(1, nf):
        project(source(k), False)

    gain = gain_ref[...].astype(F32)
    pooled_rows = []
    for s in range(2 * seqs):
        rows = slice(s * length, (s + 1) * length)
        h_rows = hid[rows, :]
        inv = lax.rsqrt(jnp.mean(h_rows * h_rows, axis=1, keepdims=True) + 1e-05)
        invs[rows, :] = jnp.broadcast_to(inv, (length, invs.shape[1]))
        pooled_rows.append(jnp.sum(h_rows * inv, axis=0, keepdims=True))
    pooled = jnp.concatenate(pooled_rows, axis=0) * (gain / length)
    scale = lax.rsqrt(jnp.sum(pooled * pooled, axis=1, keepdims=True) + 1e-06)
    unit = pooled * scale

    per = 2 * seqs
    folds = 16 // per
    fold = width // folds
    lanes = msg.shape[1] - fold
    folded = jnp.concatenate([unit[:, i * fold : (i + 1) * fold] for i in range(folds)], axis=0)
    pattern = jnp.broadcast_to(pattern_ref[...].astype(F32), (16, nd)).astype(BF16)
    allowed_row = jnp.dot(pattern, spread_ref[...], preferred_element_type=F32)
    row_id = lax.broadcasted_iota(jnp.int32, (16, lanes), 0)
    lane_id = lax.broadcasted_iota(jnp.int32, (16, lanes), 1)
    meta = jnp.where(row_id < seqs, allowed_row, 0.0)
    for s in range(seqs):
        hit = jnp.logical_and(row_id == seqs + s, lane_id == positive_ref[s : s + 1, :] + d * seqs)
        meta = jnp.where(hit, 1.0, meta)
    msg[:, :fold] = folded.astype(BF16)
    msg[:, fold:] = meta.astype(BF16)
    pool_copies = [
        send(msg, pool.at[d], lax.rem(d + s, nd), f) for s in range(1, nd)
    ]
    pool[d] = msg[...]
    for k in range(1, nf):
        ctx_copies[k - 1].wait_recv()
        ref = ctx_all.at[core, source(k)]
        sibling_ctx.append(send(ref, ref, flip(d, 1), f))
    for copy in pool_copies:
        copy.wait_recv()

    cols = nd * seqs
    x = pool[:, :, :fold].reshape(nd * 16, fold)
    info = pool[:, :, fold:].reshape(nd * 16, lanes)
    pick_q = select_ref[:cols, :]
    pick_p = select_ref[cols:, :]
    same = same_ref[...]
    gram = lax.dot_general(x, x, NT, preferred_element_type=F32) * same
    half = jnp.dot(pick_q, gram, preferred_element_type=F32, precision=HIGH)
    scores = 20.0 * lax.dot_general(
        half, pick_p, NT, preferred_element_type=F32, precision=HIGH
    )
    allowed = jnp.dot(pick_q.astype(BF16), info, preferred_element_type=F32)[:, :cols]
    onehot = jnp.dot(pick_p.astype(BF16), info, preferred_element_type=F32)[:, :cols]
    weighted = allowed * jnp.exp(scores)
    total = jnp.sum(weighted, axis=1, keepdims=True)
    losses = jnp.log(total) - jnp.sum(onehot * scores, axis=1, keepdims=True)
    coeff = (weighted / total - onehot).astype(BF16)
    col_id = lax.broadcasted_iota(jnp.int32, (cols, 1), 0)
    for s in range(seqs):
        loss_ref[s : s + 1, :] = jnp.sum(
            jnp.where(col_id == d * seqs + s, losses, 0.0), axis=0, keepdims=True
        )
    lane_col = lax.broadcasted_iota(jnp.int32, (16, cols), 1) - d * seqs
    mine_q = jnp.where(lane_col == rows_ref[0], 1.0, 0.0).astype(BF16)
    mine_p = jnp.where(lane_col == rows_ref[1], 1.0, 0.0).astype(BF16)
    coeff_q = jnp.dot(mine_q, coeff, preferred_element_type=F32).astype(BF16)
    coeff_p = lax.dot_general(mine_p, coeff, NT, preferred_element_type=F32).astype(BF16)
    mix = jnp.dot(coeff_q, pick_p.astype(BF16), preferred_element_type=F32)
    mix = mix + jnp.dot(coeff_p, pick_q.astype(BF16), preferred_element_type=F32)
    mix = (mix * same[:16, :]).astype(BF16)
    d_fold = 20.0 * jnp.dot(mix, x, preferred_element_type=F32)
    d_embed = jnp.concatenate([d_fold[i * per : (i + 1) * per, :] for i in range(folds)], axis=1)
    d_pooled = (d_embed - unit * jnp.sum(unit * d_embed, axis=1, keepdims=True)) * scale
    d_gated = d_pooled * (gain / length)

    for s in range(2 * seqs):
        rows = slice(s * length, (s + 1) * length)
        h_rows = hid[rows, :]
        inv = invs[rows, 0:1]
        gated = d_gated[s : s + 1, :]
        mean = jnp.mean(h_rows * gated, axis=1, keepdims=True)
        d_rows = inv * gated - h_rows * (inv * inv * inv * mean)
        for i in range(nz):
            for j in range(2):
                first = (4 * i + j) * bw
                second = (4 * i + 2 + j) * bw
                pair = [d_rows[:, first : first + bw], d_rows[:, second : second + bw]]
                dhs[j, i, rows, :] = jnp.concatenate(pair, axis=1).astype(BF16)

    masks = list(range(nz - 1, -1, -1))
    peers = [(dc, k) for dc in range(2) for k in range(nf) if (dc, k) != (0, 0)]
    dh_copies = {}
    for mask in masks:
        block = flip(z, mask)
        for dc, k in peers:
            dh_copies[mask, dc, k] = send(
                dhs.at[flip(core, dc), block],
                dh_all.at[core, f, block],
                flip(d, dc),
                other(k),
            )
    for copy in sibling_ctx:
        copy.wait_recv()

    row_tile = min(256, depth)
    y_copies, z_copies = {}, []

    def reduce_block(mask):
        block = flip(z, mask)
        for dc, k in peers:
            dh_copies[mask, dc, k].wait_recv()

        def step(n, carry):
            at = pl.ds(pl.multiple_of(n * row_tile, row_tile), row_tile)
            total = jnp.dot(ctx_all[core, f, at, :], dhs[core, block], preferred_element_type=F32)
            for dc, k in peers:
                a, b = flip(core, dc), source(k)
                total += jnp.dot(
                    ctx_all[a, b, at, :], dh_all[a, b, block], preferred_element_type=F32
                )
            low, high = total[:, :bw], total[:, bw:]
            y_send[mask, at, :] = jnp.where(y == 0, high, low).astype(BF16)
            kept[mask, at, :] = jnp.where(y == 0, low, high)
            return carry

        lax.fori_loop(0, depth // row_tile, step, 0)
        y_copies[mask] = send(y_send.at[mask], y_recv.at[mask], flip(d, 2), f)

    def forward_block(mask):
        y_copies[mask].wait_recv()
        z_send[mask] = (kept[mask] + y_recv[mask].astype(F32)).astype(BF16)
        z_copies.append(send(z_send.at[mask], z_recv.at[mask], flip(d, 4 * mask), f))

    for place, mask in enumerate(masks):
        reduce_block(mask)
        if place:
            forward_block(masks[place - 1])
    y_copies[0].wait_recv()
    grad = kept[0] + y_recv[0].astype(F32)
    for place, copy in enumerate(z_copies):
        copy.wait_recv()
        grad = grad + z_recv[masks[place]].astype(F32)
    grad_ref[...] = grad
    for copy in started:
        copy.wait_send()


def body(nd, nf, context, residual, weight, gain, pattern, positive):
    tokens, width = context.shape
    depth = weight.shape[0]
    seqs = positive.shape[0]
    nz = nd // 4
    bw = width // nd
    per = 2 * seqs
    folds = 16 // per
    fold = width // folds
    lanes = 128
    cols = nd * seqs
    flat = np.arange(nd * 16)
    col = np.arange(cols)[:, None]
    owner = flat[None, :] // 16 == col // seqs
    pick_q = owner & (flat[None, :] % per == col % seqs)
    pick_p = owner & (flat[None, :] % per == seqs + col % seqs)
    select = np.concatenate([pick_q, pick_p]).astype(np.float32)
    group = (flat % 16) // per
    same = (group[:, None] == group[None, :]).astype(np.float32)
    spread = (np.arange(lanes)[None, :] // seqs == np.arange(nd)[:, None]).astype(np.float32)
    row = np.broadcast_to((np.arange(16) % per)[:, None], (16, cols))
    rows = np.stack([np.where(row < seqs, row, -4096), np.where(row >= seqs, row - seqs, -4096)])
    vmem = pl.BlockSpec(memory_space=pltpu.VMEM)
    hbm = pl.BlockSpec(memory_space=pl.ANY)
    copies = count_copies(nd, nf)
    losses, grad = pl.pallas_call(
        functools.partial(kernel, nd, nf, seqs),
        out_shape=(
            jax.ShapeDtypeStruct((seqs, 1), F32),
            jax.ShapeDtypeStruct((depth, bw), F32),
        ),
        in_specs=[hbm, hbm, hbm] + [vmem] * 7,
        out_specs=(vmem, vmem),
        scratch_shapes=[
            pltpu.VMEM((tokens, width), BF16),
            pltpu.VMEM((tokens, width), BF16),
            pltpu.VMEM((nf, 8, 2, depth // 16, width), BF16),
            pltpu.VMEM((tokens, width), F32),
            pltpu.VMEM((tokens, 128), F32),
            pltpu.VMEM((nf, depth, tokens), BF16),
            pltpu.VMEM((2, nf, depth, tokens), BF16),
            pltpu.VMEM((16, fold + lanes), BF16),
            pltpu.VMEM((nd, 16, fold + lanes), BF16),
            pltpu.VMEM((2, nz, tokens, 2 * bw), BF16),
            pltpu.VMEM((2, nf, nz, tokens, 2 * bw), BF16),
            pltpu.VMEM((nz, depth, bw), BF16),
            pltpu.VMEM((nz, depth, bw), BF16),
            pltpu.VMEM((nz, depth, bw), F32),
            pltpu.VMEM((nz, depth, bw), BF16),
            pltpu.VMEM((nz, depth, bw), BF16),
            pltpu.SemaphoreType.DMA((3,)),
            pltpu.SemaphoreType.DMA((copies,)),
            pltpu.SemaphoreType.DMA((copies,)),
        ],
        compiler_params=pltpu.CompilerParams(
            collective_id=0, has_side_effects=True, vmem_limit_bytes=52 * 1024 * 1024
        ),
        cost_estimate=pl.CostEstimate(
            flops=8 * tokens * width * width, bytes_accessed=8 * depth * width, transcendentals=0
        ),
    )(
        context,
        residual,
        weight.reshape(8, 2, depth // 16, width),
        gain.reshape(1, width),
        pattern,
        positive.reshape(seqs, 1),
        jnp.asarray(spread, BF16),
        jnp.asarray(select),
        jnp.asarray(same),
        jnp.asarray(rows, jnp.int32),
    )
    return losses.reshape(seqs), grad


def solution(mesh):
    return jax.shard_map(
        functools.partial(body, mesh.shape["dp"], mesh.shape["fsdp"]),
        mesh=mesh,
        in_specs=(
            P(("dp", "fsdp"), None),
            P(("dp", "fsdp"), None),
            P("fsdp", None),
            P(),
            P(("dp", "fsdp"), None),
            P(("dp", "fsdp")),
        ),
        out_specs=(P(("dp", "fsdp")), P("fsdp", "dp")),
        check_vma=False,
    )
```

```python
import functools

import jax
import jax.numpy as jnp
from jax import lax
from jax.experimental import pallas as pl
from jax.experimental.pallas import tpu as pltpu
from jax.sharding import PartitionSpec as P

MESH = pl.DeviceIdType.MESH
F32 = jnp.float32
BF16 = jnp.bfloat16
HIGH = lax.Precision.HIGHEST
NT = (((1,), (1,)), ((), ()))


def flip(index, mask):
    out = index
    bit = 1
    while bit <= mask:
        if mask & bit:
            out = out + bit * (1 - 2 * lax.rem(lax.div(index, bit), 2))
        bit *= 2
    return out


def count_copies(nd, nf):
    nz = nd // 4
    groups = nd // 2
    weights = (nf - 1) * (4 + 2 + 5 + 5 + 16)
    return weights + (nf - 1) + nf + 4 * groups + (2 * nf - 1) * nz + nz + nz - 1


def kernel(
    nd,
    nf,
    seqs,
    context_hbm,
    residual_hbm,
    weight_hbm,
    gain_hbm,
    pattern_hbm,
    positive_ref,
    loss_ref,
    grad_ref,
    ctx,
    res,
    gain_ref,
    pattern_ref,
    wg,
    hid,
    invs,
    ctx_t,
    ctx_all,
    note,
    notes,
    msg,
    pool,
    dhs,
    dh_all,
    y_send,
    y_recv,
    kept,
    z_send,
    z_recv,
    local_sem,
    send_sem,
    recv_sem,
):
    d = lax.axis_index("dp")
    f = lax.axis_index("fsdp")
    tokens, width = ctx.shape
    depth = wg.shape[1]
    nz = nd // 4
    bw = width // nd
    core = lax.rem(d, 2)
    y = lax.rem(lax.div(d, 2), 2)
    z = lax.div(d, 4)
    spot = lax.rem(d, 8)
    length = tokens // (2 * seqs)
    parts = 4
    rows_in = depth // 8
    wide = width // parts
    other = lambda k: lax.rem(f + k, nf)
    source = lambda k: lax.rem(f + nf - k, nf)
    others = range(1, nf)

    started = []

    def send(src, dst, dd, ff):
        slot = len(started)
        copy = pltpu.make_async_remote_copy(
            src_ref=src,
            dst_ref=dst,
            send_sem=send_sem.at[slot],
            recv_sem=recv_sem.at[slot],
            device_id=(dd, ff),
            device_id_type=MESH,
        )
        copy.start()
        started.append(copy)
        return copy

    def load(src, dst, slot):
        copy = pltpu.make_async_copy(src, dst, local_sem.at[slot])
        copy.start()
        return copy

    loads = [
        load(context_hbm, ctx, 0),
        load(weight_hbm, wg.at[f], 1),
        load(residual_hbm, res, 2),
        load(gain_hbm, gain_ref, 3),
        load(pattern_hbm, pattern_ref, 4),
    ]

    barrier = pltpu.get_barrier_semaphore()
    sibling = flip(d, 1)
    partners = [(lax.rem(d + 2 * s, nd), f) for s in range(1, nd // 2)] + [(sibling, f)]
    partners += [(d, other(k)) for k in others] + [(sibling, other(k)) for k in others]
    for partner in partners:
        pl.semaphore_signal(barrier, inc=1, device_id=partner, device_id_type=MESH)
    pl.semaphore_wait(barrier, len(partners))

    near_y, near_z, far = flip(spot, 2), flip(spot, 4), flip(spot, 6)

    def piece(place, h):
        return (pl.ds(pl.multiple_of(place * rows_in, rows_in), rows_in), slice(h * wide, (h + 1) * wide))

    def fetch(place, h):
        at = piece(place, h)
        return [send(weight_hbm.at[at], wg.at[(f, *at)], d, other(k)) for k in others]

    def pass_on(place, h, mask):
        at = piece(place, h)
        copies = []
        for k in others:
            ref = wg.at[(source(k), *at)]
            copies.append(send(ref, ref, flip(d, mask), f))
        return copies

    def arrive(copies):
        for copy in copies:
            copy.wait_recv()

    direct = {0: fetch(spot, 0), 1: fetch(spot, 1)}

    loads[4].wait()
    lanes = note.shape[1]
    lane_id = lax.broadcasted_iota(jnp.int32, (16, lanes), 1)
    row_id = lax.broadcasted_iota(jnp.int32, (16, lanes), 0)
    log_s = seqs.bit_length() - 1
    spread_lane = lax.broadcasted_iota(jnp.int32, (nd, lanes), 1) >> log_s
    spread = spread_lane == lax.broadcasted_iota(jnp.int32, (nd, lanes), 0)
    pattern = jnp.broadcast_to(pattern_ref[...].astype(F32), (16, nd)).astype(BF16)
    allowed_row = jnp.dot(
        pattern, jnp.where(spread, 1.0, 0.0).astype(BF16), preferred_element_type=F32
    )
    meta = jnp.where(row_id < seqs, allowed_row, 0.0)
    for s in range(seqs):
        hit = jnp.logical_and(row_id == seqs + s, lane_id == positive_ref[s] + d * seqs)
        meta = jnp.where(hit, 1.0, meta)
    note[...] = meta.astype(BF16)
    notes[d] = note[...]
    near = [lax.rem(d + 2 * s, nd) for s in range(1, nd // 2)]
    behind = [lax.rem(d + nd - 2 * s, nd) for s in range(1, nd // 2)]
    note_copies = [send(note, notes.at[d], there, f) for there in near]
    note_pairs = [send(note, notes.at[d], sibling, f)]

    loads[0].wait()
    for part in range(nf):
        ctx_t[part] = ctx[:, part * depth : (part + 1) * depth].T
    ctx_all[core, f] = ctx_t[f]
    sibling_ctx = [send(ctx_all.at[core, f], ctx_all.at[core, f], sibling, f)]
    loads[1].wait()
    loads[2].wait()
    tile = 256

    def project(shard, first, start, count):
        def step(n, carry):
            cols = pl.ds(pl.multiple_of(n * tile, tile), tile)
            left = ctx[:, pl.ds(pl.multiple_of(shard * depth, 128), depth)]
            before = res[:, cols].astype(F32) if first else hid[:, cols]
            hid[:, cols] = before + jnp.dot(left, wg[shard, :, cols], preferred_element_type=F32)
            return carry

        lax.fori_loop(start // tile, (start + count) // tile, step, 0)

    arrive(direct[0])
    to_y, to_z, to_core, straight = {}, {}, {h: [] for h in range(parts)}, {}

    def spread_out(h):
        to_y[h] = pass_on(spot, h, 2)
        to_z[h] = pass_on(spot, h, 4)
        to_core[h] += pass_on(spot, h, 1)

    def finish(h):
        arrive(to_core[h])
        for k in others:
            project(source(k), False, h * wide, wide)

    spread_out(0)
    direct[2], straight[2] = fetch(spot, 2), fetch(far, 2)
    project(f, True, 0, width)
    arrive(direct[1])
    spread_out(1)
    direct[3], straight[3] = fetch(spot, 3), fetch(far, 3)
    arrive(to_z[0])
    across_y = pass_on(near_z, 0, 2)
    to_core[0] += pass_on(near_z, 0, 1)
    arrive(to_y[0])
    to_core[0] += pass_on(near_y, 0, 1)
    arrive(direct[2])
    spread_out(2)
    arrive(to_y[1])
    across_z = pass_on(near_y, 1, 4)
    to_core[1] += pass_on(near_y, 1, 1)
    arrive(to_z[1])
    to_core[1] += pass_on(near_z, 1, 1)
    arrive(straight[2])
    to_core[2] += pass_on(far, 2, 1)
    arrive(across_y)
    to_core[0] += pass_on(far, 0, 1)
    arrive(direct[3])
    spread_out(3)
    ctx_copies = [send(ctx_t.at[other(k)], ctx_all.at[core, f], d, other(k)) for k in others]
    finish(0)
    arrive(across_z)
    to_core[1] += pass_on(far, 1, 1)
    arrive(to_y[2])
    to_core[2] += pass_on(near_y, 2, 1)
    arrive(to_z[2])
    to_core[2] += pass_on(near_z, 2, 1)
    arrive(straight[3])
    to_core[3] += pass_on(far, 3, 1)
    finish(1)
    finish(2)
    arrive(to_y[3])
    to_core[3] += pass_on(near_y, 3, 1)
    arrive(to_z[3])
    to_core[3] += pass_on(near_z, 3, 1)
    for copy, origin in zip(note_copies, behind):
        copy.wait_recv()
        note_pairs.append(send(notes.at[origin], notes.at[origin], sibling, f))
    finish(3)

    loads[3].wait()
    gain = gain_ref[...].astype(F32).reshape(1, width)
    pooled_rows = []
    for s in range(2 * seqs):
        rows = slice(s * length, (s + 1) * length)
        h_rows = hid[rows, :]
        inv = lax.rsqrt(jnp.mean(h_rows * h_rows, axis=1, keepdims=True) + 1e-05)
        invs[rows, :] = jnp.broadcast_to(inv, (length, invs.shape[1]))
        pooled_rows.append(jnp.sum(h_rows * inv, axis=0, keepdims=True))
    pooled = jnp.concatenate(pooled_rows, axis=0) * (gain / length)
    scale = lax.rsqrt(jnp.sum(pooled * pooled, axis=1, keepdims=True) + 1e-06)
    unit = pooled * scale
    per = 2 * seqs
    folds = 16 // per
    fold = width // folds
    folded = jnp.concatenate([unit[:, i * fold : (i + 1) * fold] for i in range(folds)], axis=0)
    msg[...] = folded.astype(BF16)
    pool_copies = [send(msg, pool.at[d], there, f) for there in near]
    pool_pairs = [send(msg, pool.at[d], sibling, f)]
    pool[d] = msg[...]

    cols = nd * seqs
    total_rows = nd * 16
    log_p = per.bit_length() - 1
    flat = lax.broadcasted_iota(jnp.int32, (cols, total_rows), 1)
    col = lax.broadcasted_iota(jnp.int32, (cols, total_rows), 0)
    owner = (flat >> 4) == (col >> log_s)
    inner, slot_in = flat & (per - 1), col & (seqs - 1)
    pick_q = jnp.where(jnp.logical_and(owner, inner == slot_in), 1.0, 0.0)
    pick_p = jnp.where(jnp.logical_and(owner, inner == slot_in + seqs), 1.0, 0.0)
    row_fold = (lax.broadcasted_iota(jnp.int32, (total_rows, total_rows), 0) & 15) >> log_p
    col_fold = (lax.broadcasted_iota(jnp.int32, (total_rows, total_rows), 1) & 15) >> log_p
    same = jnp.where(row_fold == col_fold, 1.0, 0.0)
    lane_col = lax.broadcasted_iota(jnp.int32, (16, cols), 1) - d * seqs
    row_in = lax.broadcasted_iota(jnp.int32, (16, cols), 0) & (per - 1)
    hit_q = jnp.logical_and(lane_col == row_in, row_in < seqs)
    hit_p = jnp.logical_and(lane_col + seqs == row_in, row_in >= seqs)
    mine_q = jnp.where(hit_q, 1.0, 0.0).astype(BF16)
    mine_p = jnp.where(hit_p, 1.0, 0.0).astype(BF16)
    arrive(note_pairs)
    info = notes[...].reshape(total_rows, lanes)
    allowed = jnp.dot(pick_q.astype(BF16), info, preferred_element_type=F32)[:, :cols]
    onehot = jnp.dot(pick_p.astype(BF16), info, preferred_element_type=F32)[:, :cols]

    for copy, origin in zip(pool_copies, behind):
        copy.wait_recv()
        pool_pairs.append(send(pool.at[origin], pool.at[origin], sibling, f))
    for k in others:
        ctx_copies[k - 1].wait_recv()
        ref = ctx_all.at[core, source(k)]
        sibling_ctx.append(send(ref, ref, sibling, f))
    arrive(pool_pairs)

    x = pool[...].reshape(total_rows, fold)
    gram = lax.dot_general(x, x, NT, preferred_element_type=F32) * same
    half = jnp.dot(pick_q, gram, preferred_element_type=F32, precision=HIGH)
    scores = 20.0 * lax.dot_general(
        half, pick_p, NT, preferred_element_type=F32, precision=HIGH
    )
    weighted = allowed * jnp.exp(scores)
    total = jnp.sum(weighted, axis=1, keepdims=True)
    losses = jnp.log(total) - jnp.sum(onehot * scores, axis=1, keepdims=True)
    coeff = (weighted / total - onehot).astype(BF16)
    coeff_q = jnp.dot(mine_q, coeff, preferred_element_type=F32).astype(BF16)
    coeff_p = lax.dot_general(mine_p, coeff, NT, preferred_element_type=F32).astype(BF16)
    mix = jnp.dot(coeff_q, pick_p.astype(BF16), preferred_element_type=F32)
    mix = mix + jnp.dot(coeff_p, pick_q.astype(BF16), preferred_element_type=F32)
    mix = (mix * same[:16, :]).astype(BF16)
    d_fold = 20.0 * jnp.dot(mix, x, preferred_element_type=F32)
    d_embed = jnp.concatenate([d_fold[i * per : (i + 1) * per, :] for i in range(folds)], axis=1)
    d_pooled = (d_embed - unit * jnp.sum(unit * d_embed, axis=1, keepdims=True)) * scale
    d_gated = d_pooled * (gain / length)

    for s in range(2 * seqs):
        rows = slice(s * length, (s + 1) * length)
        h_rows = hid[rows, :]
        inv = invs[rows, 0:1]
        gated = d_gated[s : s + 1, :]
        mean = jnp.mean(h_rows * gated, axis=1, keepdims=True)
        d_rows = inv * gated - h_rows * (inv * inv * inv * mean)
        for i in range(nz):
            for j in range(2):
                first = (4 * i + j) * bw
                second = (4 * i + 2 + j) * bw
                pair = [d_rows[:, first : first + bw], d_rows[:, second : second + bw]]
                dhs[j, i, rows, :] = jnp.concatenate(pair, axis=1).astype(BF16)

    masks = list(range(nz - 1, -1, -1))
    peers = [(dc, k) for dc in range(2) for k in range(nf) if (dc, k) != (0, 0)]
    dh_copies = {}

    def share(mask):
        block = flip(z, mask)
        for dc, k in peers:
            dh_copies[mask, dc, k] = send(
                dhs.at[flip(core, dc), block],
                dh_all.at[core, f, block],
                flip(d, dc),
                other(k),
            )

    for mask in masks[:2]:
        share(mask)
    col_id = lax.broadcasted_iota(jnp.int32, (cols, 1), 0)
    for s in range(seqs):
        loss_ref[s] = jnp.sum(jnp.where(col_id == d * seqs + s, losses, 0.0))
    arrive(sibling_ctx)

    row_tile = min(256, depth)
    y_copies, z_copies = {}, {}

    def reduce_block(place, mask):
        block = flip(z, mask)
        for dc, k in peers:
            dh_copies[mask, dc, k].wait_recv()
        if place + 2 < nz:
            share(masks[place + 2])

        def step(n, carry):
            at = pl.ds(pl.multiple_of(n * row_tile, row_tile), row_tile)
            total = jnp.dot(ctx_all[core, f, at, :], dhs[core, block], preferred_element_type=F32)
            for dc, k in peers:
                a, b = flip(core, dc), source(k)
                total += jnp.dot(
                    ctx_all[a, b, at, :], dh_all[a, b, block], preferred_element_type=F32
                )
            low, high = total[:, :bw], total[:, bw:]
            y_send[mask, at, :] = jnp.where(y == 0, high, low).astype(BF16)
            kept[mask, at, :] = jnp.where(y == 0, low, high)
            return carry

        lax.fori_loop(0, depth // row_tile, step, 0)
        y_copies[mask] = send(y_send.at[mask], y_recv.at[mask], flip(d, 2), f)

    def forward_block(mask):
        y_copies[mask].wait_recv()
        summed = kept[mask] + y_recv[mask].astype(F32)
        bit = 1
        while bit < nz and not mask & bit:
            z_copies[mask | bit].wait_recv()
            summed = summed + z_recv[mask | bit].astype(F32)
            bit *= 2
        if mask:
            z_send[mask] = summed.astype(BF16)
            z_copies[mask] = send(z_send.at[mask], z_recv.at[mask], flip(d, 4 * bit), f)
        else:
            grad_ref[...] = summed

    for place, mask in enumerate(masks):
        reduce_block(place, mask)
        if place:
            forward_block(masks[place - 1])
    forward_block(0)
    for copy in started:
        copy.wait_send()


def body(nd, nf, context, residual, weight, gain, pattern, positive):
    tokens, width = context.shape
    depth = weight.shape[0]
    seqs = positive.shape[0]
    nz = nd // 4
    bw = width // nd
    fold = width * 2 * seqs // 16
    lanes = 128
    vmem = pl.BlockSpec(memory_space=pltpu.VMEM)
    smem = pl.BlockSpec(memory_space=pltpu.SMEM)
    hbm = pl.BlockSpec(memory_space=pl.ANY)
    copies = count_copies(nd, nf)
    return pl.pallas_call(
        functools.partial(kernel, nd, nf, seqs),
        out_shape=(
            jax.ShapeDtypeStruct((seqs,), F32),
            jax.ShapeDtypeStruct((depth, bw), F32),
        ),
        in_specs=[hbm] * 5 + [smem],
        out_specs=(smem, vmem),
        scratch_shapes=[
            pltpu.VMEM((tokens, width), BF16),
            pltpu.VMEM((tokens, width), BF16),
            pltpu.VMEM((width,), BF16),
            pltpu.VMEM((1, nd), jnp.int32),
            pltpu.VMEM((nf, depth, width), BF16),
            pltpu.VMEM((tokens, width), F32),
            pltpu.VMEM((tokens, 128), F32),
            pltpu.VMEM((nf, depth, tokens), BF16),
            pltpu.VMEM((2, nf, depth, tokens), BF16),
            pltpu.VMEM((16, lanes), BF16),
            pltpu.VMEM((nd, 16, lanes), BF16),
            pltpu.VMEM((16, fold), BF16),
            pltpu.VMEM((nd, 16, fold), BF16),
            pltpu.VMEM((2, nz, tokens, 2 * bw), BF16),
            pltpu.VMEM((2, nf, nz, tokens, 2 * bw), BF16),
            pltpu.VMEM((nz, depth, bw), BF16),
            pltpu.VMEM((nz, depth, bw), BF16),
            pltpu.VMEM((nz, depth, bw), F32),
            pltpu.VMEM((nz, depth, bw), BF16),
            pltpu.VMEM((nz, depth, bw), BF16),
            pltpu.SemaphoreType.DMA((5,)),
            pltpu.SemaphoreType.DMA((copies,)),
            pltpu.SemaphoreType.DMA((copies,)),
        ],
        compiler_params=pltpu.CompilerParams(
            collective_id=0, has_side_effects=True, vmem_limit_bytes=52 * 1024 * 1024
        ),
        cost_estimate=pl.CostEstimate(
            flops=8 * tokens * width * width, bytes_accessed=8 * depth * width, transcendentals=0
        ),
    )(context, residual, weight, gain, pattern, positive)


def solution(mesh):
    return jax.shard_map(
        functools.partial(body, mesh.shape["dp"], mesh.shape["fsdp"]),
        mesh=mesh,
        in_specs=(
            P(("dp", "fsdp"), None),
            P(("dp", "fsdp"), None),
            P("fsdp", None),
            P(),
            P(("dp", "fsdp"), None),
            P(("dp", "fsdp")),
        ),
        out_specs=(P(("dp", "fsdp")), P("fsdp", "dp")),
        check_vma=False,
    )
```

```python
import functools

import jax
import jax.numpy as jnp
from jax import lax
from jax.experimental import pallas as pl
from jax.experimental.pallas import tpu as pltpu
from jax.sharding import PartitionSpec as P

MESH = pl.DeviceIdType.MESH
F32 = jnp.float32
BF16 = jnp.bfloat16
HIGH = lax.Precision.HIGHEST
NT = (((1,), (1,)), ((), ()))


def flip(index, mask):
    out = index
    bit = 1
    while bit <= mask:
        if mask & bit:
            out = out + bit * (1 - 2 * lax.rem(lax.div(index, bit), 2))
        bit *= 2
    return out


def count_copies(nd, nf):
    nz = nd // 4
    groups = nd // 2
    weights = (nf - 1) * (4 + 2 + 5 + 5 + 16)
    return weights + (nf - 1) + nf + 4 * groups + (2 * nf - 1) * (nz + 2) + nz + nz - 1


def kernel(
    nd,
    nf,
    seqs,
    context_hbm,
    residual_hbm,
    weight_hbm,
    gain_hbm,
    pattern_hbm,
    positive_hbm,
    loss_ref,
    grad_ref,
    ctx,
    res,
    gain_ref,
    pattern_ref,
    positive_ref,
    wg,
    hid,
    invs,
    ctx_t,
    ctx_all,
    note,
    notes,
    msg,
    pool,
    hs,
    hs_all,
    gs,
    gs_all,
    tok,
    tok_all,
    weights,
    dh,
    y_send,
    y_recv,
    kept,
    z_send,
    z_recv,
    local_sem,
    send_sem,
    recv_sem,
):
    d = lax.axis_index("dp")
    f = lax.axis_index("fsdp")
    tokens, width = ctx.shape
    depth = wg.shape[1]
    nz = nd // 4
    bw = width // nd
    core = lax.rem(d, 2)
    y = lax.rem(lax.div(d, 2), 2)
    z = lax.div(d, 4)
    spot = lax.rem(d, 8)
    length = tokens // (2 * seqs)
    parts = 4
    rows_in = depth // 8
    wide = width // parts
    other = lambda k: lax.rem(f + k, nf)
    source = lambda k: lax.rem(f + nf - k, nf)
    others = range(1, nf)

    started = []

    def send(src, dst, dd, ff):
        slot = len(started)
        copy = pltpu.make_async_remote_copy(
            src_ref=src,
            dst_ref=dst,
            send_sem=send_sem.at[slot],
            recv_sem=recv_sem.at[slot],
            device_id=(dd, ff),
            device_id_type=MESH,
        )
        copy.start()
        started.append(copy)
        return copy

    def load(src, dst, slot):
        copy = pltpu.make_async_copy(src, dst, local_sem.at[slot])
        copy.start()
        return copy

    loads = [
        load(context_hbm, ctx, 0),
        load(weight_hbm, wg.at[f], 1),
        load(residual_hbm, res, 2),
        load(gain_hbm, gain_ref, 3),
        load(pattern_hbm, pattern_ref, 4),
        load(positive_hbm, positive_ref, 5),
    ]

    barrier = pltpu.get_barrier_semaphore()
    sibling = flip(d, 1)
    partners = [(lax.rem(d + 2 * s, nd), f) for s in range(1, nd // 2)] + [(sibling, f)]
    partners += [(d, other(k)) for k in others] + [(sibling, other(k)) for k in others]
    for partner in partners:
        pl.semaphore_signal(barrier, inc=1, device_id=partner, device_id_type=MESH)
    pl.semaphore_wait(barrier, len(partners))

    near_y, near_z, far = flip(spot, 2), flip(spot, 4), flip(spot, 6)

    def piece(place, h):
        return (pl.ds(pl.multiple_of(place * rows_in, rows_in), rows_in), slice(h * wide, (h + 1) * wide))

    def fetch(place, h):
        at = piece(place, h)
        return [send(weight_hbm.at[at], wg.at[(f, *at)], d, other(k)) for k in others]

    def pass_on(place, h, mask):
        at = piece(place, h)
        copies = []
        for k in others:
            ref = wg.at[(source(k), *at)]
            copies.append(send(ref, ref, flip(d, mask), f))
        return copies

    def arrive(copies):
        for copy in copies:
            copy.wait_recv()

    direct = {0: fetch(spot, 0), 1: fetch(spot, 1)}

    loads[4].wait()
    loads[5].wait()
    lanes = note.shape[1]
    lane_id = lax.broadcasted_iota(jnp.int32, (16, lanes), 1)
    row_id = lax.broadcasted_iota(jnp.int32, (16, lanes), 0)
    log_s = seqs.bit_length() - 1
    spread_lane = lax.broadcasted_iota(jnp.int32, (nd, lanes), 1) >> log_s
    spread = spread_lane == lax.broadcasted_iota(jnp.int32, (nd, lanes), 0)
    pattern = jnp.broadcast_to(pattern_ref[...].astype(F32), (16, nd)).astype(BF16)
    allowed_row = jnp.dot(
        pattern, jnp.where(spread, 1.0, 0.0).astype(BF16), preferred_element_type=F32
    )
    meta = jnp.where(row_id < seqs, allowed_row, 0.0)
    for s in range(seqs):
        hit = jnp.logical_and(row_id == seqs + s, lane_id == positive_ref[s] + d * seqs)
        meta = jnp.where(hit, 1.0, meta)
    note[...] = meta.astype(BF16)
    notes[d] = note[...]
    near = [lax.rem(d + 2 * s, nd) for s in range(1, nd // 2)]
    behind = [lax.rem(d + nd - 2 * s, nd) for s in range(1, nd // 2)]
    note_copies = [send(note, notes.at[d], there, f) for there in near]
    note_pairs = [send(note, notes.at[d], sibling, f)]

    loads[0].wait()
    for part in range(nf):
        ctx_t[part] = ctx[:, part * depth : (part + 1) * depth].T
    ctx_all[core, f] = ctx_t[f]
    sibling_ctx = [send(ctx_all.at[core, f], ctx_all.at[core, f], sibling, f)]
    loads[1].wait()
    loads[2].wait()
    tile = 256

    def project(shard, first, start, count):
        def step(n, carry):
            cols = pl.ds(pl.multiple_of(n * tile, tile), tile)
            left = ctx[:, pl.ds(pl.multiple_of(shard * depth, 128), depth)]
            before = res[:, cols].astype(F32) if first else hid[:, cols]
            hid[:, cols] = before + jnp.dot(left, wg[shard, :, cols], preferred_element_type=F32)
            return carry

        lax.fori_loop(start // tile, (start + count) // tile, step, 0)

    arrive(direct[0])
    to_y, to_z, to_core, straight = {}, {}, {h: [] for h in range(parts)}, {}

    def spread_out(h):
        to_y[h] = pass_on(spot, h, 2)
        to_z[h] = pass_on(spot, h, 4)
        to_core[h] += pass_on(spot, h, 1)

    def finish(h):
        arrive(to_core[h])
        for k in others:
            project(source(k), False, h * wide, wide)
        for i in range(h * nz // parts, (h + 1) * nz // parts):
            for j in range(2):
                first, second = (4 * i + j) * bw, (4 * i + 2 + j) * bw
                pair = [hid[:, first : first + bw], hid[:, second : second + bw]]
                hs[j, i] = jnp.concatenate(pair, axis=1).astype(BF16)

    spread_out(0)
    direct[2], straight[2] = fetch(spot, 2), fetch(far, 2)
    project(f, True, 0, width)
    arrive(direct[1])
    spread_out(1)
    direct[3], straight[3] = fetch(spot, 3), fetch(far, 3)
    arrive(to_z[0])
    across_y = pass_on(near_z, 0, 2)
    to_core[0] += pass_on(near_z, 0, 1)
    arrive(to_y[0])
    to_core[0] += pass_on(near_y, 0, 1)
    arrive(direct[2])
    spread_out(2)
    arrive(to_y[1])
    across_z = pass_on(near_y, 1, 4)
    to_core[1] += pass_on(near_y, 1, 1)
    arrive(to_z[1])
    to_core[1] += pass_on(near_z, 1, 1)
    arrive(straight[2])
    to_core[2] += pass_on(far, 2, 1)
    arrive(across_y)
    to_core[0] += pass_on(far, 0, 1)
    arrive(direct[3])
    spread_out(3)
    ctx_copies = [send(ctx_t.at[other(k)], ctx_all.at[core, f], d, other(k)) for k in others]
    finish(0)
    arrive(across_z)
    to_core[1] += pass_on(far, 1, 1)
    arrive(to_y[2])
    to_core[2] += pass_on(near_y, 2, 1)
    arrive(to_z[2])
    to_core[2] += pass_on(near_z, 2, 1)
    arrive(straight[3])
    to_core[3] += pass_on(far, 3, 1)
    finish(1)
    finish(2)
    arrive(to_y[3])
    to_core[3] += pass_on(near_y, 3, 1)
    arrive(to_z[3])
    to_core[3] += pass_on(near_z, 3, 1)
    for copy, origin in zip(note_copies, behind):
        copy.wait_recv()
        note_pairs.append(send(notes.at[origin], notes.at[origin], sibling, f))
    finish(3)

    masks = list(range(nz - 1, -1, -1))
    peers = [(dc, k) for dc in range(2) for k in range(nf) if (dc, k) != (0, 0)]
    dh_copies = {}

    def share(mask):
        block = flip(z, mask)
        for dc, k in peers:
            dh_copies[mask, dc, k] = send(
                hs.at[flip(core, dc), block],
                hs_all.at[core, f, block],
                flip(d, dc),
                other(k),
            )

    share(masks[0])

    loads[3].wait()
    gain = gain_ref[...].astype(F32).reshape(1, width)
    pooled_rows = []
    for s in range(2 * seqs):
        rows = slice(s * length, (s + 1) * length)
        h_rows = hid[rows, :]
        inv = lax.rsqrt(jnp.mean(h_rows * h_rows, axis=1, keepdims=True) + 1e-05)
        invs[rows, :] = jnp.broadcast_to(inv, (length, invs.shape[1]))
        pooled_rows.append(jnp.sum(h_rows * inv, axis=0, keepdims=True))
    pooled = jnp.concatenate(pooled_rows, axis=0) * (gain / length)
    scale = lax.rsqrt(jnp.sum(pooled * pooled, axis=1, keepdims=True) + 1e-06)
    unit = pooled * scale
    per = 2 * seqs
    folds = 16 // per
    fold = width // folds
    folded = jnp.concatenate([unit[:, i * fold : (i + 1) * fold] for i in range(folds)], axis=0)
    msg[...] = folded.astype(BF16)
    pool_copies = [send(msg, pool.at[d], there, f) for there in near]
    pool_pairs = [send(msg, pool.at[d], sibling, f)]
    pool[d] = msg[...]
    share(masks[1])

    cols = nd * seqs
    total_rows = nd * 16
    log_p = per.bit_length() - 1
    flat = lax.broadcasted_iota(jnp.int32, (cols, total_rows), 1)
    col = lax.broadcasted_iota(jnp.int32, (cols, total_rows), 0)
    owner = (flat >> 4) == (col >> log_s)
    inner, slot_in = flat & (per - 1), col & (seqs - 1)
    pick_q = jnp.where(jnp.logical_and(owner, inner == slot_in), 1.0, 0.0)
    pick_p = jnp.where(jnp.logical_and(owner, inner == slot_in + seqs), 1.0, 0.0)
    row_fold = (lax.broadcasted_iota(jnp.int32, (total_rows, total_rows), 0) & 15) >> log_p
    col_fold = (lax.broadcasted_iota(jnp.int32, (total_rows, total_rows), 1) & 15) >> log_p
    same = jnp.where(row_fold == col_fold, 1.0, 0.0)
    lane_col = lax.broadcasted_iota(jnp.int32, (16, cols), 1) - d * seqs
    row_in = lax.broadcasted_iota(jnp.int32, (16, cols), 0) & (per - 1)
    hit_q = jnp.logical_and(lane_col == row_in, row_in < seqs)
    hit_p = jnp.logical_and(lane_col + seqs == row_in, row_in >= seqs)
    mine_q = jnp.where(hit_q, 1.0, 0.0).astype(BF16)
    mine_p = jnp.where(hit_p, 1.0, 0.0).astype(BF16)
    arrive(note_pairs)
    info = notes[...].reshape(total_rows, lanes)
    allowed = jnp.dot(pick_q.astype(BF16), info, preferred_element_type=F32)[:, :cols]
    onehot = jnp.dot(pick_p.astype(BF16), info, preferred_element_type=F32)[:, :cols]

    for copy, origin in zip(pool_copies, behind):
        copy.wait_recv()
        pool_pairs.append(send(pool.at[origin], pool.at[origin], sibling, f))
    for k in others:
        ctx_copies[k - 1].wait_recv()
        ref = ctx_all.at[core, source(k)]
        sibling_ctx.append(send(ref, ref, sibling, f))
    arrive(pool_pairs)
    share(masks[2])

    x = pool[...].reshape(total_rows, fold)
    gram = lax.dot_general(x, x, NT, preferred_element_type=F32) * same
    half = jnp.dot(pick_q, gram, preferred_element_type=F32, precision=HIGH)
    scores = 20.0 * lax.dot_general(
        half, pick_p, NT, preferred_element_type=F32, precision=HIGH
    )
    weighted = allowed * jnp.exp(scores)
    total = jnp.sum(weighted, axis=1, keepdims=True)
    losses = jnp.log(total) - jnp.sum(onehot * scores, axis=1, keepdims=True)
    coeff = (weighted / total - onehot).astype(BF16)
    coeff_q = jnp.dot(mine_q, coeff, preferred_element_type=F32).astype(BF16)
    coeff_p = lax.dot_general(mine_p, coeff, NT, preferred_element_type=F32).astype(BF16)
    mix = jnp.dot(coeff_q, pick_p.astype(BF16), preferred_element_type=F32)
    mix = mix + jnp.dot(coeff_p, pick_q.astype(BF16), preferred_element_type=F32)
    mix = (mix * same[:16, :]).astype(BF16)
    d_fold = 20.0 * jnp.dot(mix, x, preferred_element_type=F32)
    d_embed = jnp.concatenate([d_fold[i * per : (i + 1) * per, :] for i in range(folds)], axis=1)
    d_pooled = (d_embed - unit * jnp.sum(unit * d_embed, axis=1, keepdims=True)) * scale
    d_gated = d_pooled * (gain / length)

    for i in range(nz):
        for j in range(2):
            first, second = (4 * i + j) * bw, (4 * i + 2 + j) * bw
            pair = [d_gated[:, first : first + bw], d_gated[:, second : second + bw]]
            at = (i % 2) * 4
            gs[j, i // 2, at : at + per, :] = jnp.concatenate(pair, axis=1)
    gs_copies = {}
    for dc, k in peers:
        gs_copies[dc, k] = send(gs.at[flip(core, dc)], gs_all.at[core, f], flip(d, dc), other(k))
    lane = lax.broadcasted_iota(jnp.int32, (length, 128), 1)
    for s in range(2 * seqs):
        rows = slice(s * length, (s + 1) * length)
        inv = invs[rows, 0:1]
        mean = jnp.mean(hid[rows, :] * d_gated[s : s + 1, :], axis=1, keepdims=True)
        weights[0, rows, :] = jnp.where(lane < 4, inv, inv * inv * inv * mean)
    tok[...] = weights[0].T[:8, :]
    tok_copies = {}
    for dc, k in peers:
        tok_copies[dc, k] = send(tok, tok_all.at[core, f], flip(d, dc), other(k))
    col_id = lax.broadcasted_iota(jnp.int32, (cols, 1), 0)
    for s in range(seqs):
        loss_ref[s] = jnp.sum(jnp.where(col_id == d * seqs + s, losses, 0.0))
    arrive(sibling_ctx)

    row_tile = min(256, depth)
    y_copies, z_copies = {}, {}

    for index, (dc, k) in enumerate(peers):
        gs_copies[dc, k].wait_recv()
        tok_copies[dc, k].wait_recv()
        rows8 = tok_all[flip(core, dc), source(k)]
        weights[index + 1] = jnp.concatenate([rows8] * 16, axis=0).T

    def differentiate(index, h_block, gated, odd):
        picked = jnp.where(odd == 1, gated[4 : 4 + per, :], gated[:per, :])
        spread_rows = jnp.concatenate(
            [jnp.broadcast_to(picked[s : s + 1, :], (length, 2 * bw)) for s in range(per)], axis=0
        )
        inv, slope = weights[index, :, 0:1], weights[index, :, 4:5]
        dh[index] = (inv * spread_rows - h_block.astype(F32) * slope).astype(BF16)

    def reduce_block(place, mask):
        block = flip(z, mask)
        half_block, odd = lax.div(block, 2), lax.rem(block, 2)
        differentiate(0, hs[core, block], gs[core, half_block], odd)
        for index, (dc, k) in enumerate(peers):
            a, b = flip(core, dc), source(k)
            dh_copies[mask, dc, k].wait_recv()
            differentiate(index + 1, hs_all[a, b, block], gs_all[a, b, half_block], odd)
        if place + 3 < nz:
            share(masks[place + 3])

        def step(n, carry):
            at = pl.ds(pl.multiple_of(n * row_tile, row_tile), row_tile)
            total = jnp.dot(ctx_all[core, f, at, :], dh[0], preferred_element_type=F32)
            for index, (dc, k) in enumerate(peers):
                a, b = flip(core, dc), source(k)
                total += jnp.dot(ctx_all[a, b, at, :], dh[index + 1], preferred_element_type=F32)
            low, high = total[:, :bw], total[:, bw:]
            y_send[mask, at, :] = jnp.where(y == 0, high, low).astype(BF16)
            kept[mask, at, :] = jnp.where(y == 0, low, high)
            return carry

        lax.fori_loop(0, depth // row_tile, step, 0)
        y_copies[mask] = send(y_send.at[mask], y_recv.at[mask], flip(d, 2), f)

    def forward_block(mask):
        y_copies[mask].wait_recv()
        summed = kept[mask] + y_recv[mask].astype(F32)
        bit = 1
        while bit < nz and not mask & bit:
            z_copies[mask | bit].wait_recv()
            summed = summed + z_recv[mask | bit].astype(F32)
            bit *= 2
        if mask:
            z_send[mask] = summed.astype(BF16)
            z_copies[mask] = send(z_send.at[mask], z_recv.at[mask], flip(d, 4 * bit), f)
        else:
            grad_ref[...] = summed

    for place, mask in enumerate(masks):
        reduce_block(place, mask)
        if place:
            forward_block(masks[place - 1])
    forward_block(0)
    for copy in started:
        copy.wait_send()


def body(nd, nf, context, residual, weight, gain, pattern, positive):
    tokens, width = context.shape
    depth = weight.shape[0]
    seqs = positive.shape[0]
    nz = nd // 4
    bw = width // nd
    fold = width * 2 * seqs // 16
    lanes = 128
    vmem = pl.BlockSpec(memory_space=pltpu.VMEM)
    smem = pl.BlockSpec(memory_space=pltpu.SMEM)
    hbm = pl.BlockSpec(memory_space=pl.ANY)
    copies = count_copies(nd, nf)
    return pl.pallas_call(
        functools.partial(kernel, nd, nf, seqs),
        out_shape=(
            jax.ShapeDtypeStruct((seqs,), F32),
            jax.ShapeDtypeStruct((depth, bw), F32),
        ),
        in_specs=[hbm] * 6,
        out_specs=(smem, vmem),
        scratch_shapes=[
            pltpu.VMEM((tokens, width), BF16),
            pltpu.VMEM((tokens, width), BF16),
            pltpu.VMEM((width,), BF16),
            pltpu.VMEM((1, nd), jnp.int32),
            pltpu.SMEM((seqs,), jnp.int32),
            pltpu.VMEM((nf, depth, width), BF16),
            pltpu.VMEM((tokens, width), F32),
            pltpu.VMEM((tokens, 128), F32),
            pltpu.VMEM((nf, depth, tokens), BF16),
            pltpu.VMEM((2, nf, depth, tokens), BF16),
            pltpu.VMEM((16, lanes), BF16),
            pltpu.VMEM((nd, 16, lanes), BF16),
            pltpu.VMEM((16, fold), BF16),
            pltpu.VMEM((nd, 16, fold), BF16),
            pltpu.VMEM((2, nz, tokens, 2 * bw), BF16),
            pltpu.VMEM((2, nf, nz, tokens, 2 * bw), BF16),
            pltpu.VMEM((2, nz // 2, 8, 2 * bw), F32),
            pltpu.VMEM((2, nf, nz // 2, 8, 2 * bw), F32),
            pltpu.VMEM((8, tokens), F32),
            pltpu.VMEM((2, nf, 8, tokens), F32),
            pltpu.VMEM((2 * nf, tokens, 128), F32),
            pltpu.VMEM((2 * nf, tokens, 2 * bw), BF16),
            pltpu.VMEM((nz, depth, bw), BF16),
            pltpu.VMEM((nz, depth, bw), BF16),
            pltpu.VMEM((nz, depth, bw), F32),
            pltpu.VMEM((nz, depth, bw), BF16),
            pltpu.VMEM((nz, depth, bw), BF16),
            pltpu.SemaphoreType.DMA((6,)),
            pltpu.SemaphoreType.DMA((copies,)),
            pltpu.SemaphoreType.DMA((copies,)),
        ],
        compiler_params=pltpu.CompilerParams(
            collective_id=0, has_side_effects=True, vmem_limit_bytes=63 * 1024 * 1024
        ),
        cost_estimate=pl.CostEstimate(
            flops=8 * tokens * width * width, bytes_accessed=8 * depth * width, transcendentals=0
        ),
    )(context, residual, weight, gain, pattern, positive)


def solution(mesh):
    return jax.shard_map(
        functools.partial(body, mesh.shape["dp"], mesh.shape["fsdp"]),
        mesh=mesh,
        in_specs=(
            P(("dp", "fsdp"), None),
            P(("dp", "fsdp"), None),
            P("fsdp", None),
            P(),
            P(("dp", "fsdp"), None),
            P(("dp", "fsdp")),
        ),
        out_specs=(P(("dp", "fsdp")), P("fsdp", "dp")),
        check_vma=False,
    )
```

```python
import functools

import jax
import jax.numpy as jnp
from jax import lax
from jax.experimental import pallas as pl
from jax.experimental.pallas import tpu as pltpu
from jax.sharding import PartitionSpec as P

MESH = pl.DeviceIdType.MESH
F32 = jnp.float32
BF16 = jnp.bfloat16
HIGH = lax.Precision.HIGHEST
NT = (((1,), (1,)), ((), ()))


def flip(index, mask):
    out = index
    bit = 1
    while bit <= mask:
        if mask & bit:
            out = out + bit * (1 - 2 * lax.rem(lax.div(index, bit), 2))
        bit *= 2
    return out


def count_copies(nd, nf):
    nz = nd // 4
    groups = nd // 2
    weights = (nf - 1) * (4 + 2 + 5 + 5 + 16)
    return weights + 16 * (nf - 1) + 1 + 4 * groups + (2 * nf - 1) * nz + nz + nz - 1


def kernel(
    nd,
    nf,
    seqs,
    context_hbm,
    residual_hbm,
    weight_hbm,
    gain_hbm,
    pattern_hbm,
    positive_ref,
    loss_ref,
    grad_ref,
    ctx,
    res,
    gain_ref,
    pattern_ref,
    wg,
    hid,
    invs,
    slopes,
    g_rows,
    ctx_t,
    ctx_all,
    note,
    notes,
    msg,
    pool,
    dhs,
    dh_all,
    y_send,
    y_recv,
    kept,
    z_send,
    z_recv,
    local_sem,
    send_sem,
    recv_sem,
):
    d = lax.axis_index("dp")
    f = lax.axis_index("fsdp")
    tokens, width = ctx.shape
    depth = wg.shape[1]
    nz = nd // 4
    bw = width // nd
    core = lax.rem(d, 2)
    y = lax.rem(lax.div(d, 2), 2)
    z = lax.div(d, 4)
    spot = lax.rem(d, 8)
    length = tokens // (2 * seqs)
    parts = 4
    rows_in = depth // 8
    wide = width // parts
    other = lambda k: lax.rem(f + k, nf)
    source = lambda k: lax.rem(f + nf - k, nf)
    others = range(1, nf)

    started = []

    def send(src, dst, dd, ff):
        slot = len(started)
        copy = pltpu.make_async_remote_copy(
            src_ref=src,
            dst_ref=dst,
            send_sem=send_sem.at[slot],
            recv_sem=recv_sem.at[slot],
            device_id=(dd, ff),
            device_id_type=MESH,
        )
        copy.start()
        started.append(copy)
        return copy

    def load(src, dst, slot):
        copy = pltpu.make_async_copy(src, dst, local_sem.at[slot])
        copy.start()
        return copy

    loads = [
        load(context_hbm, ctx, 0),
        load(weight_hbm, wg.at[f], 1),
        load(residual_hbm, res, 2),
        load(gain_hbm, gain_ref, 3),
        load(pattern_hbm, pattern_ref, 4),
    ]

    barrier = pltpu.get_barrier_semaphore()
    sibling = flip(d, 1)
    partners = [(lax.rem(d + 2 * s, nd), f) for s in range(1, nd // 2)] + [(sibling, f)]
    partners += [(d, other(k)) for k in others] + [(sibling, other(k)) for k in others]
    for partner in partners:
        pl.semaphore_signal(barrier, inc=1, device_id=partner, device_id_type=MESH)
    pl.semaphore_wait(barrier, len(partners))

    near_y, near_z, far = flip(spot, 2), flip(spot, 4), flip(spot, 6)

    def piece(place, h):
        return (pl.ds(pl.multiple_of(place * rows_in, rows_in), rows_in), slice(h * wide, (h + 1) * wide))

    def fetch(place, h):
        at = piece(place, h)
        return [send(weight_hbm.at[at], wg.at[(f, *at)], d, other(k)) for k in others]

    def pass_on(place, h, mask):
        at = piece(place, h)
        copies = []
        for k in others:
            ref = wg.at[(source(k), *at)]
            copies.append(send(ref, ref, flip(d, mask), f))
        return copies

    def arrive(copies):
        for copy in copies:
            copy.wait_recv()

    direct = {0: fetch(spot, 0), 1: fetch(spot, 1)}

    loads[4].wait()
    lanes = note.shape[1]
    lane_id = lax.broadcasted_iota(jnp.int32, (16, lanes), 1)
    row_id = lax.broadcasted_iota(jnp.int32, (16, lanes), 0)
    log_s = seqs.bit_length() - 1
    spread_lane = lax.broadcasted_iota(jnp.int32, (nd, lanes), 1) >> log_s
    spread = spread_lane == lax.broadcasted_iota(jnp.int32, (nd, lanes), 0)
    pattern = jnp.broadcast_to(pattern_ref[...].astype(F32), (16, nd)).astype(BF16)
    allowed_row = jnp.dot(
        pattern, jnp.where(spread, 1.0, 0.0).astype(BF16), preferred_element_type=F32
    )
    meta = jnp.where(row_id < seqs, allowed_row, 0.0)
    for s in range(seqs):
        hit = jnp.logical_and(row_id == seqs + s, lane_id == positive_ref[s] + d * seqs)
        meta = jnp.where(hit, 1.0, meta)
    note[...] = meta.astype(BF16)
    notes[d] = note[...]
    near = [lax.rem(d + 2 * s, nd) for s in range(1, nd // 2)]
    behind = [lax.rem(d + nd - 2 * s, nd) for s in range(1, nd // 2)]
    note_copies = [send(note, notes.at[d], there, f) for there in near]
    note_pairs = [send(note, notes.at[d], sibling, f)]

    loads[0].wait()
    for part in range(nf):
        ctx_t[part] = ctx[:, part * depth : (part + 1) * depth].T
    ctx_all[core, f] = ctx_t[f]
    sibling_ctx = [send(ctx_all.at[core, f], ctx_all.at[core, f], sibling, f)]
    loads[1].wait()
    loads[2].wait()
    tile = 256

    def project(shard, first, start, count):
        def step(n, carry):
            cols = pl.ds(pl.multiple_of(n * tile, tile), tile)
            left = ctx[:, pl.ds(pl.multiple_of(shard * depth, 128), depth)]
            before = res[:, cols].astype(F32) if first else hid[:, cols]
            hid[:, cols] = before + jnp.dot(left, wg[shard, :, cols], preferred_element_type=F32)
            return carry

        lax.fori_loop(start // tile, (start + count) // tile, step, 0)

    arrive(direct[0])
    to_y, to_z, to_core, straight = {}, {}, {h: [] for h in range(parts)}, {}

    def spread_out(h):
        to_y[h] = pass_on(spot, h, 2)
        to_z[h] = pass_on(spot, h, 4)
        to_core[h] += pass_on(spot, h, 1)

    def finish(h):
        arrive(to_core[h])
        for k in others:
            project(source(k), False, h * wide, wide)

    chunks = 8
    ctx_copies = {}

    def chunk(i):
        return slice(i * depth // chunks, (i + 1) * depth // chunks)

    def trickle(i):
        for k in others:
            src, dst = ctx_t.at[other(k), chunk(i)], ctx_all.at[core, f, chunk(i)]
            ctx_copies[i, k] = send(src, dst, d, other(k))

    def relay(i):
        for k in others:
            ctx_copies[i, k].wait_recv()
            ref = ctx_all.at[core, source(k), chunk(i)]
            sibling_ctx.append(send(ref, ref, sibling, f))

    spread_out(0)
    direct[2], straight[2] = fetch(spot, 2), fetch(far, 2)
    project(f, True, 0, width)
    arrive(direct[1])
    spread_out(1)
    direct[3], straight[3] = fetch(spot, 3), fetch(far, 3)
    arrive(to_z[0])
    across_y = pass_on(near_z, 0, 2)
    to_core[0] += pass_on(near_z, 0, 1)
    arrive(to_y[0])
    to_core[0] += pass_on(near_y, 0, 1)
    arrive(direct[2])
    spread_out(2)
    arrive(to_y[1])
    across_z = pass_on(near_y, 1, 4)
    to_core[1] += pass_on(near_y, 1, 1)
    arrive(to_z[1])
    to_core[1] += pass_on(near_z, 1, 1)
    arrive(straight[2])
    to_core[2] += pass_on(far, 2, 1)
    arrive(across_y)
    to_core[0] += pass_on(far, 0, 1)
    arrive(direct[3])
    spread_out(3)
    trickle(0)
    finish(0)
    trickle(1)
    arrive(across_z)
    to_core[1] += pass_on(far, 1, 1)
    arrive(to_y[2])
    to_core[2] += pass_on(near_y, 2, 1)
    arrive(to_z[2])
    to_core[2] += pass_on(near_z, 2, 1)
    arrive(straight[3])
    to_core[3] += pass_on(far, 3, 1)
    trickle(2)
    finish(1)
    trickle(3)
    finish(2)
    arrive(to_y[3])
    to_core[3] += pass_on(near_y, 3, 1)
    arrive(to_z[3])
    to_core[3] += pass_on(near_z, 3, 1)
    for copy, origin in zip(note_copies, behind):
        copy.wait_recv()
        note_pairs.append(send(notes.at[origin], notes.at[origin], sibling, f))
    trickle(4)
    finish(3)

    loads[3].wait()
    gain = gain_ref[...].astype(F32).reshape(1, width)
    pooled_rows = []
    for s in range(2 * seqs):
        rows = slice(s * length, (s + 1) * length)
        h_rows = hid[rows, :]
        inv = lax.rsqrt(jnp.mean(h_rows * h_rows, axis=1, keepdims=True) + 1e-05)
        invs[rows, :] = jnp.broadcast_to(inv, (length, invs.shape[1]))
        pooled_rows.append(jnp.sum(h_rows * inv, axis=0, keepdims=True))
    pooled = jnp.concatenate(pooled_rows, axis=0) * (gain / length)
    scale = lax.rsqrt(jnp.sum(pooled * pooled, axis=1, keepdims=True) + 1e-06)
    unit = pooled * scale
    per = 2 * seqs
    folds = 16 // per
    fold = width // folds
    folded = jnp.concatenate([unit[:, i * fold : (i + 1) * fold] for i in range(folds)], axis=0)
    msg[...] = folded.astype(BF16)
    pool_copies = [send(msg, pool.at[d], there, f) for there in near]
    pool_pairs = [send(msg, pool.at[d], sibling, f)]
    pool[d] = msg[...]

    cols = nd * seqs
    total_rows = nd * 16
    log_p = per.bit_length() - 1
    flat = lax.broadcasted_iota(jnp.int32, (cols, total_rows), 1)
    col = lax.broadcasted_iota(jnp.int32, (cols, total_rows), 0)
    owner = (flat >> 4) == (col >> log_s)
    inner, slot_in = flat & (per - 1), col & (seqs - 1)
    pick_q = jnp.where(jnp.logical_and(owner, inner == slot_in), 1.0, 0.0)
    pick_p = jnp.where(jnp.logical_and(owner, inner == slot_in + seqs), 1.0, 0.0)
    row_fold = (lax.broadcasted_iota(jnp.int32, (total_rows, total_rows), 0) & 15) >> log_p
    col_fold = (lax.broadcasted_iota(jnp.int32, (total_rows, total_rows), 1) & 15) >> log_p
    same = jnp.where(row_fold == col_fold, 1.0, 0.0)
    lane_col = lax.broadcasted_iota(jnp.int32, (16, cols), 1) - d * seqs
    row_in = lax.broadcasted_iota(jnp.int32, (16, cols), 0) & (per - 1)
    hit_q = jnp.logical_and(lane_col == row_in, row_in < seqs)
    hit_p = jnp.logical_and(lane_col + seqs == row_in, row_in >= seqs)
    mine_q = jnp.where(hit_q, 1.0, 0.0).astype(BF16)
    mine_p = jnp.where(hit_p, 1.0, 0.0).astype(BF16)
    arrive(note_pairs)
    info = notes[...].reshape(total_rows, lanes)
    allowed = jnp.dot(pick_q.astype(BF16), info, preferred_element_type=F32)[:, :cols]
    onehot = jnp.dot(pick_p.astype(BF16), info, preferred_element_type=F32)[:, :cols]

    for copy, origin in zip(pool_copies, behind):
        copy.wait_recv()
        pool_pairs.append(send(pool.at[origin], pool.at[origin], sibling, f))
    for i in range(5, 8):
        trickle(i)
    for i in range(5):
        relay(i)
    arrive(pool_pairs)

    x = pool[...].reshape(total_rows, fold)
    gram = lax.dot_general(x, x, NT, preferred_element_type=F32) * same
    half = jnp.dot(pick_q, gram, preferred_element_type=F32, precision=HIGH)
    scores = 20.0 * lax.dot_general(
        half, pick_p, NT, preferred_element_type=F32, precision=HIGH
    )
    weighted = allowed * jnp.exp(scores)
    total = jnp.sum(weighted, axis=1, keepdims=True)
    losses = jnp.log(total) - jnp.sum(onehot * scores, axis=1, keepdims=True)
    coeff = (weighted / total - onehot).astype(BF16)
    coeff_q = jnp.dot(mine_q, coeff, preferred_element_type=F32).astype(BF16)
    coeff_p = lax.dot_general(mine_p, coeff, NT, preferred_element_type=F32).astype(BF16)
    mix = jnp.dot(coeff_q, pick_p.astype(BF16), preferred_element_type=F32)
    mix = mix + jnp.dot(coeff_p, pick_q.astype(BF16), preferred_element_type=F32)
    mix = (mix * same[:16, :]).astype(BF16)
    d_fold = 20.0 * jnp.dot(mix, x, preferred_element_type=F32)
    d_embed = jnp.concatenate([d_fold[i * per : (i + 1) * per, :] for i in range(folds)], axis=1)
    d_pooled = (d_embed - unit * jnp.sum(unit * d_embed, axis=1, keepdims=True)) * scale
    d_gated = d_pooled * (gain / length)

    g_rows[0:per, :] = d_gated
    for s in range(per):
        rows = slice(s * length, (s + 1) * length)
        inv = invs[rows, 0:1]
        mean = jnp.mean(hid[rows, :] * d_gated[s : s + 1, :], axis=1, keepdims=True)
        slopes[rows, :] = jnp.broadcast_to(inv * inv * inv * mean, (length, slopes.shape[1]))

    def differentiate(block):
        at = pl.ds(pl.multiple_of(block * 4 * bw, 128), 4 * bw)
        for s in range(per):
            rows = slice(s * length, (s + 1) * length)
            inv, slope = invs[rows, 0:1], slopes[rows, 0:1]
            d_rows = inv * g_rows[s : s + 1, at] - hid[rows, at] * slope
            for j in range(2):
                pair = [d_rows[:, j * bw : (j + 1) * bw], d_rows[:, (2 + j) * bw : (3 + j) * bw]]
                dhs[j, block, rows, :] = jnp.concatenate(pair, axis=1).astype(BF16)

    masks = list(range(nz - 1, -1, -1))
    peers = [(dc, k) for dc in range(2) for k in range(nf) if (dc, k) != (0, 0)]
    dh_copies = {}

    def share(mask):
        block = flip(z, mask)
        for dc, k in peers:
            dh_copies[mask, dc, k] = send(
                dhs.at[flip(core, dc), block],
                dh_all.at[core, f, block],
                flip(d, dc),
                other(k),
            )

    for place, mask in enumerate(masks):
        differentiate(flip(z, mask))
        if place < 2:
            share(mask)
    for i in range(5, 8):
        relay(i)
    col_id = lax.broadcasted_iota(jnp.int32, (cols, 1), 0)
    for s in range(seqs):
        loss_ref[s] = jnp.sum(jnp.where(col_id == d * seqs + s, losses, 0.0))
    arrive(sibling_ctx)

    row_tile = min(256, depth)
    y_copies, z_copies = {}, {}

    def reduce_block(place, mask):
        block = flip(z, mask)
        for dc, k in peers:
            dh_copies[mask, dc, k].wait_recv()
        if place + 2 < nz:
            share(masks[place + 2])

        def step(n, carry):
            at = pl.ds(pl.multiple_of(n * row_tile, row_tile), row_tile)
            total = jnp.dot(ctx_all[core, f, at, :], dhs[core, block], preferred_element_type=F32)
            for dc, k in peers:
                a, b = flip(core, dc), source(k)
                total += jnp.dot(
                    ctx_all[a, b, at, :], dh_all[a, b, block], preferred_element_type=F32
                )
            low, high = total[:, :bw], total[:, bw:]
            y_send[mask, at, :] = jnp.where(y == 0, high, low).astype(BF16)
            kept[mask, at, :] = jnp.where(y == 0, low, high)
            return carry

        lax.fori_loop(0, depth // row_tile, step, 0)
        y_copies[mask] = send(y_send.at[mask], y_recv.at[mask], flip(d, 2), f)

    def forward_block(mask):
        y_copies[mask].wait_recv()
        summed = kept[mask] + y_recv[mask].astype(F32)
        bit = 1
        while bit < nz and not mask & bit:
            z_copies[mask | bit].wait_recv()
            summed = summed + z_recv[mask | bit].astype(F32)
            bit *= 2
        if mask:
            z_send[mask] = summed.astype(BF16)
            z_copies[mask] = send(z_send.at[mask], z_recv.at[mask], flip(d, 4 * bit), f)
        else:
            grad_ref[...] = summed

    for place, mask in enumerate(masks):
        reduce_block(place, mask)
        if place:
            forward_block(masks[place - 1])
    forward_block(0)
    for copy in started:
        copy.wait_send()


def body(nd, nf, context, residual, weight, gain, pattern, positive):
    tokens, width = context.shape
    depth = weight.shape[0]
    seqs = positive.shape[0]
    nz = nd // 4
    bw = width // nd
    fold = width * 2 * seqs // 16
    lanes = 128
    vmem = pl.BlockSpec(memory_space=pltpu.VMEM)
    smem = pl.BlockSpec(memory_space=pltpu.SMEM)
    hbm = pl.BlockSpec(memory_space=pl.ANY)
    copies = count_copies(nd, nf)
    return pl.pallas_call(
        functools.partial(kernel, nd, nf, seqs),
        out_shape=(
            jax.ShapeDtypeStruct((seqs,), F32),
            jax.ShapeDtypeStruct((depth, bw), F32),
        ),
        in_specs=[hbm] * 5 + [smem],
        out_specs=(smem, vmem),
        scratch_shapes=[
            pltpu.VMEM((tokens, width), BF16),
            pltpu.VMEM((tokens, width), BF16),
            pltpu.VMEM((width,), BF16),
            pltpu.VMEM((1, nd), jnp.int32),
            pltpu.VMEM((nf, depth, width), BF16),
            pltpu.VMEM((tokens, width), F32),
            pltpu.VMEM((tokens, 128), F32),
            pltpu.VMEM((tokens, 128), F32),
            pltpu.VMEM((8, width), F32),
            pltpu.VMEM((nf, depth, tokens), BF16),
            pltpu.VMEM((2, nf, depth, tokens), BF16),
            pltpu.VMEM((16, lanes), BF16),
            pltpu.VMEM((nd, 16, lanes), BF16),
            pltpu.VMEM((16, fold), BF16),
            pltpu.VMEM((nd, 16, fold), BF16),
            pltpu.VMEM((2, nz, tokens, 2 * bw), BF16),
            pltpu.VMEM((2, nf, nz, tokens, 2 * bw), BF16),
            pltpu.VMEM((nz, depth, bw), BF16),
            pltpu.VMEM((nz, depth, bw), BF16),
            pltpu.VMEM((nz, depth, bw), F32),
            pltpu.VMEM((nz, depth, bw), BF16),
            pltpu.VMEM((nz, depth, bw), BF16),
            pltpu.SemaphoreType.DMA((5,)),
            pltpu.SemaphoreType.DMA((copies,)),
            pltpu.SemaphoreType.DMA((copies,)),
        ],
        compiler_params=pltpu.CompilerParams(
            collective_id=0, has_side_effects=True, vmem_limit_bytes=63 * 1024 * 1024
        ),
        cost_estimate=pl.CostEstimate(
            flops=8 * tokens * width * width, bytes_accessed=8 * depth * width, transcendentals=0
        ),
    )(context, residual, weight, gain, pattern, positive)


def solution(mesh):
    return jax.shard_map(
        functools.partial(body, mesh.shape["dp"], mesh.shape["fsdp"]),
        mesh=mesh,
        in_specs=(
            P(("dp", "fsdp"), None),
            P(("dp", "fsdp"), None),
            P("fsdp", None),
            P(),
            P(("dp", "fsdp"), None),
            P(("dp", "fsdp")),
        ),
        out_specs=(P(("dp", "fsdp")), P("fsdp", "dp")),
        check_vma=False,
    )
```

```python
import functools

import jax
import jax.numpy as jnp
from jax import lax
from jax.experimental import pallas as pl
from jax.experimental.pallas import tpu as pltpu
from jax.sharding import PartitionSpec as P

MESH = pl.DeviceIdType.MESH
F32 = jnp.float32
BF16 = jnp.bfloat16
NT = (((1,), (1,)), ((), ()))


def flip(index, mask):
    out = index
    bit = 1
    while bit <= mask:
        if mask & bit:
            out = out + bit * (1 - 2 * lax.rem(lax.div(index, bit), 2))
        bit *= 2
    return out


def count_copies(nd, nf):
    nz = nd // 4
    groups = nd // 2
    weights = (nf - 1) * (4 + 2 + 5 + 5 + 16)
    return weights + 16 * (nf - 1) + 1 + 4 * groups + (2 * nf - 1) * 2 * nz + nz + nz - 1


def kernel(
    nd,
    nf,
    seqs,
    context_hbm,
    residual_hbm,
    weight_hbm,
    gain_hbm,
    pattern_hbm,
    positive_ref,
    loss_ref,
    grad_ref,
    ctx,
    res,
    gain_ref,
    pattern_ref,
    wg,
    hid,
    invs,
    slopes,
    g_rows,
    ctx_t,
    ctx_all,
    note,
    notes,
    msg,
    pool,
    dhs,
    dh_all,
    y_send,
    y_recv,
    kept,
    z_send,
    z_recv,
    local_sem,
    send_sem,
    recv_sem,
):
    d = lax.axis_index("dp")
    f = lax.axis_index("fsdp")
    tokens, width = ctx.shape
    depth = wg.shape[1]
    nz = nd // 4
    bw = width // nd
    core = lax.rem(d, 2)
    y = lax.rem(lax.div(d, 2), 2)
    z = lax.div(d, 4)
    spot = lax.rem(d, 8)
    length = tokens // (2 * seqs)
    parts = 4
    rows_in = depth // 8
    wide = width // parts
    other = lambda k: lax.rem(f + k, nf)
    source = lambda k: lax.rem(f + nf - k, nf)
    others = range(1, nf)

    started = []

    def send(src, dst, dd, ff):
        slot = len(started)
        copy = pltpu.make_async_remote_copy(
            src_ref=src,
            dst_ref=dst,
            send_sem=send_sem.at[slot],
            recv_sem=recv_sem.at[slot],
            device_id=(dd, ff),
            device_id_type=MESH,
        )
        copy.start()
        started.append(copy)
        return copy

    def load(src, dst, slot):
        copy = pltpu.make_async_copy(src, dst, local_sem.at[slot])
        copy.start()
        return copy

    loads = [
        load(context_hbm, ctx, 0),
        load(weight_hbm, wg.at[f], 1),
        load(residual_hbm, res, 2),
        load(gain_hbm, gain_ref, 3),
        load(pattern_hbm, pattern_ref, 4),
    ]

    barrier = pltpu.get_barrier_semaphore()
    sibling = flip(d, 1)
    partners = [(lax.rem(d + 2 * s, nd), f) for s in range(1, nd // 2)] + [(sibling, f)]
    partners += [(d, other(k)) for k in others] + [(sibling, other(k)) for k in others]
    for partner in partners:
        pl.semaphore_signal(barrier, inc=1, device_id=partner, device_id_type=MESH)
    pl.semaphore_wait(barrier, len(partners))

    near_y, near_z, far = flip(spot, 2), flip(spot, 4), flip(spot, 6)

    def piece(place, h):
        return (pl.ds(pl.multiple_of(place * rows_in, rows_in), rows_in), slice(h * wide, (h + 1) * wide))

    def fetch(place, h):
        at = piece(place, h)
        return [send(weight_hbm.at[at], wg.at[(f, *at)], d, other(k)) for k in others]

    def pass_on(place, h, mask):
        at = piece(place, h)
        copies = []
        for k in others:
            ref = wg.at[(source(k), *at)]
            copies.append(send(ref, ref, flip(d, mask), f))
        return copies

    def arrive(copies):
        for copy in copies:
            copy.wait_recv()

    direct = {0: fetch(spot, 0)}

    loads[4].wait()
    lanes = note.shape[1]
    lane_id = lax.broadcasted_iota(jnp.int32, (16, lanes), 1)
    row_id = lax.broadcasted_iota(jnp.int32, (16, lanes), 0)
    log_s = seqs.bit_length() - 1
    spread_lane = lax.broadcasted_iota(jnp.int32, (nd, lanes), 1) >> log_s
    spread = spread_lane == lax.broadcasted_iota(jnp.int32, (nd, lanes), 0)
    pattern = jnp.broadcast_to(pattern_ref[...].astype(F32), (16, nd)).astype(BF16)
    allowed_row = jnp.dot(
        pattern, jnp.where(spread, 1.0, 0.0).astype(BF16), preferred_element_type=F32
    )
    meta = jnp.where(row_id < seqs, allowed_row, 0.0)
    for s in range(seqs):
        hit = jnp.logical_and(row_id == seqs + s, lane_id == positive_ref[s] + d * seqs)
        meta = jnp.where(hit, 1.0, meta)
    note[...] = meta.astype(BF16)
    notes[d] = note[...]
    near = [lax.rem(d + 2 * s, nd) for s in range(1, nd // 2)]
    behind = [lax.rem(d + nd - 2 * s, nd) for s in range(1, nd // 2)]
    note_copies = [send(note, notes.at[d], there, f) for there in near]
    note_pairs = [send(note, notes.at[d], sibling, f)]

    loads[0].wait()
    for part in range(nf):
        ctx_t[part] = ctx[:, part * depth : (part + 1) * depth].T
    direct[1] = fetch(spot, 1)
    ctx_all[core, f] = ctx_t[f]
    sibling_ctx = [send(ctx_all.at[core, f], ctx_all.at[core, f], sibling, f)]
    loads[1].wait()
    loads[2].wait()
    tile = 256

    def project(shard, first, start, count):
        def step(n, carry):
            cols = pl.ds(pl.multiple_of(n * tile, tile), tile)
            left = ctx[:, pl.ds(pl.multiple_of(shard * depth, 128), depth)]
            before = res[:, cols].astype(F32) if first else hid[:, cols]
            hid[:, cols] = before + jnp.dot(left, wg[shard, :, cols], preferred_element_type=F32)
            return carry

        lax.fori_loop(start // tile, (start + count) // tile, step, 0)

    arrive(direct[0])
    to_y, to_z, to_core, straight = {}, {}, {h: [] for h in range(parts)}, {}

    def spread_out(h):
        to_y[h] = pass_on(spot, h, 2)
        to_z[h] = pass_on(spot, h, 4)
        to_core[h] += pass_on(spot, h, 1)

    def finish(h):
        arrive(to_core[h])
        for k in others:
            project(source(k), False, h * wide, wide)

    chunks = 8
    ctx_copies = {}

    def chunk(i):
        return slice(i * depth // chunks, (i + 1) * depth // chunks)

    def trickle(i):
        for k in others:
            src, dst = ctx_t.at[other(k), chunk(i)], ctx_all.at[core, f, chunk(i)]
            ctx_copies[i, k] = send(src, dst, d, other(k))

    def relay(i):
        for k in others:
            ctx_copies[i, k].wait_recv()
            ref = ctx_all.at[core, source(k), chunk(i)]
            sibling_ctx.append(send(ref, ref, sibling, f))

    spread_out(0)
    direct[2], straight[2] = fetch(spot, 2), fetch(far, 2)
    project(f, True, 0, width)
    arrive(direct[1])
    spread_out(1)
    direct[3], straight[3] = fetch(spot, 3), fetch(far, 3)
    arrive(to_z[0])
    across_y = pass_on(near_z, 0, 2)
    to_core[0] += pass_on(near_z, 0, 1)
    arrive(to_y[0])
    to_core[0] += pass_on(near_y, 0, 1)
    arrive(direct[2])
    spread_out(2)
    arrive(to_y[1])
    across_z = pass_on(near_y, 1, 4)
    to_core[1] += pass_on(near_y, 1, 1)
    arrive(to_z[1])
    to_core[1] += pass_on(near_z, 1, 1)
    arrive(straight[2])
    to_core[2] += pass_on(far, 2, 1)
    arrive(across_y)
    to_core[0] += pass_on(far, 0, 1)
    arrive(direct[3])
    spread_out(3)
    trickle(0)
    finish(0)
    trickle(1)
    arrive(across_z)
    to_core[1] += pass_on(far, 1, 1)
    arrive(to_y[2])
    to_core[2] += pass_on(near_y, 2, 1)
    arrive(to_z[2])
    to_core[2] += pass_on(near_z, 2, 1)
    arrive(straight[3])
    to_core[3] += pass_on(far, 3, 1)
    trickle(2)
    finish(1)
    trickle(3)
    finish(2)
    arrive(to_y[3])
    to_core[3] += pass_on(near_y, 3, 1)
    arrive(to_z[3])
    to_core[3] += pass_on(near_z, 3, 1)
    for copy, origin in zip(note_copies, behind):
        copy.wait_recv()
        note_pairs.append(send(notes.at[origin], notes.at[origin], sibling, f))
    trickle(4)
    finish(3)

    loads[3].wait()
    gain = gain_ref[...].astype(F32).reshape(1, width)
    pooled_rows = []
    for s in range(2 * seqs):
        rows = slice(s * length, (s + 1) * length)
        h_rows = hid[rows, :]
        inv = lax.rsqrt(jnp.mean(h_rows * h_rows, axis=1, keepdims=True) + 1e-05)
        invs[rows, :] = jnp.broadcast_to(inv, (length, invs.shape[1]))
        pooled_rows.append(jnp.sum(h_rows * inv, axis=0, keepdims=True))
    pooled = jnp.concatenate(pooled_rows, axis=0) * (gain / length)
    scale = lax.rsqrt(jnp.sum(pooled * pooled, axis=1, keepdims=True) + 1e-06)
    unit = pooled * scale
    per = 2 * seqs
    folds = 16 // per
    fold = width // folds
    folded = jnp.concatenate([unit[:, i * fold : (i + 1) * fold] for i in range(folds)], axis=0)
    msg[...] = folded.astype(BF16)
    pool_copies = [send(msg, pool.at[d], there, f) for there in near]
    pool_pairs = [send(msg, pool.at[d], sibling, f)]
    pool[d] = msg[...]

    cols = nd * seqs
    total_rows = nd * 16
    log_p = per.bit_length() - 1
    flat = lax.broadcasted_iota(jnp.int32, (cols, total_rows), 1)
    col = lax.broadcasted_iota(jnp.int32, (cols, total_rows), 0)
    owner = (flat >> 4) == (col >> log_s)
    inner, slot_in = flat & (per - 1), col & (seqs - 1)
    pick_q = jnp.where(jnp.logical_and(owner, inner == slot_in), 1.0, 0.0).astype(BF16)
    pick_p = jnp.where(jnp.logical_and(owner, inner == slot_in + seqs), 1.0, 0.0).astype(BF16)
    row_fold = (lax.broadcasted_iota(jnp.int32, (total_rows, total_rows), 0) & 15) >> log_p
    col_fold = (lax.broadcasted_iota(jnp.int32, (total_rows, total_rows), 1) & 15) >> log_p
    same = jnp.where(row_fold == col_fold, 1.0, 0.0)
    lane_col = lax.broadcasted_iota(jnp.int32, (16, cols), 1) - d * seqs
    row_in = lax.broadcasted_iota(jnp.int32, (16, cols), 0) & (per - 1)
    hit_q = jnp.logical_and(lane_col == row_in, row_in < seqs)
    hit_p = jnp.logical_and(lane_col + seqs == row_in, row_in >= seqs)
    mine_q = jnp.where(hit_q, 1.0, 0.0).astype(BF16)
    mine_p = jnp.where(hit_p, 1.0, 0.0).astype(BF16)
    arrive(note_pairs)
    info = notes[...].reshape(total_rows, lanes)
    allowed = jnp.dot(pick_q, info, preferred_element_type=F32)[:, :cols]
    onehot = jnp.dot(pick_p, info, preferred_element_type=F32)[:, :cols]

    for copy, origin in zip(pool_copies, behind):
        copy.wait_recv()
        pool_pairs.append(send(pool.at[origin], pool.at[origin], sibling, f))
    for i in range(5, 8):
        trickle(i)
    for i in range(5):
        relay(i)
    arrive(pool_pairs)

    def three(value):
        high = value.astype(BF16)
        rest = value - high.astype(F32)
        middle = rest.astype(BF16)
        return high, middle, (rest - middle.astype(F32)).astype(BF16)

    x = pool[...].reshape(total_rows, fold)
    gram = lax.dot_general(x, x, NT, preferred_element_type=F32) * same
    half = sum(jnp.dot(pick_q, part, preferred_element_type=F32) for part in three(gram))
    scores = 20.0 * sum(
        lax.dot_general(part, pick_p, NT, preferred_element_type=F32) for part in three(half)
    )
    weighted = allowed * jnp.exp(scores)
    total = jnp.sum(weighted, axis=1, keepdims=True)
    losses = jnp.log(total) - jnp.sum(onehot * scores, axis=1, keepdims=True)
    coeff = (weighted / total - onehot).astype(BF16)
    coeff_q = jnp.dot(mine_q, coeff, preferred_element_type=F32).astype(BF16)
    coeff_p = lax.dot_general(mine_p, coeff, NT, preferred_element_type=F32).astype(BF16)
    mix = jnp.dot(coeff_q, pick_p, preferred_element_type=F32)
    mix = mix + jnp.dot(coeff_p, pick_q, preferred_element_type=F32)
    mix = (mix * same[:16, :]).astype(BF16)
    d_fold = 20.0 * jnp.dot(mix, x, preferred_element_type=F32)
    d_embed = jnp.concatenate([d_fold[i * per : (i + 1) * per, :] for i in range(folds)], axis=1)
    d_pooled = (d_embed - unit * jnp.sum(unit * d_embed, axis=1, keepdims=True)) * scale
    d_gated = d_pooled * (gain / length)

    g_rows[0:per, :] = d_gated
    for s in range(per):
        rows = slice(s * length, (s + 1) * length)
        inv = invs[rows, 0:1]
        mean = jnp.mean(hid[rows, :] * d_gated[s : s + 1, :], axis=1, keepdims=True)
        slopes[rows, :] = jnp.broadcast_to(inv * inv * inv * mean, (length, slopes.shape[1]))

    def differentiate(block):
        at = pl.ds(pl.multiple_of(block * 4 * bw, 128), 4 * bw)
        for s in range(per):
            rows = slice(s * length, (s + 1) * length)
            inv, slope = invs[rows, 0:1], slopes[rows, 0:1]
            d_rows = inv * g_rows[s : s + 1, at] - hid[rows, at] * slope
            for j in range(4):
                dhs[j % 2, block, j // 2, rows, :] = d_rows[:, j * bw : (j + 1) * bw].astype(BF16)

    masks = list(range(nz - 1, -1, -1))
    peers = [(dc, k) for dc in range(2) for k in range(nf) if (dc, k) != (0, 0)]
    dh_copies = {}
    halves = [(mask, away) for mask in masks for away in (1, 0)]

    def share(mask, away):
        block, side = flip(z, mask), flip(y, away)
        for dc, k in peers:
            dh_copies[mask, away, dc, k] = send(
                dhs.at[flip(core, dc), block, side],
                dh_all.at[core, f, block, side],
                flip(d, dc),
                other(k),
            )

    for place, mask in enumerate(masks):
        differentiate(flip(z, mask))
        if place < 2:
            share(*halves[place])
    for i in range(5, 8):
        relay(i)
    col_id = lax.broadcasted_iota(jnp.int32, (cols, 1), 0)
    for s in range(seqs):
        loss_ref[s] = jnp.sum(jnp.where(col_id == d * seqs + s, losses, 0.0))
    arrive(sibling_ctx)

    row_tile = min(256, depth)
    y_copies, z_copies = {}, {}

    def reduce_half(place):
        mask, away = halves[place]
        block, side = flip(z, mask), flip(y, away)
        for dc, k in peers:
            dh_copies[mask, away, dc, k].wait_recv()
        if place + 2 < len(halves):
            share(*halves[place + 2])

        def step(n, carry):
            at = pl.ds(pl.multiple_of(n * row_tile, row_tile), row_tile)
            total = jnp.dot(
                ctx_all[core, f, at, :], dhs[core, block, side], preferred_element_type=F32
            )
            for dc, k in peers:
                a, b = flip(core, dc), source(k)
                total += jnp.dot(
                    ctx_all[a, b, at, :], dh_all[a, b, block, side], preferred_element_type=F32
                )
            if away:
                y_send[mask, at, :] = total.astype(BF16)
            else:
                kept[mask, at, :] = total
            return carry

        lax.fori_loop(0, depth // row_tile, step, 0)
        if away:
            y_copies[mask] = send(y_send.at[mask], y_recv.at[mask], flip(d, 2), f)

    def forward_block(mask):
        y_copies[mask].wait_recv()
        summed = kept[mask] + y_recv[mask].astype(F32)
        bit = 1
        while bit < nz and not mask & bit:
            z_copies[mask | bit].wait_recv()
            summed = summed + z_recv[mask | bit].astype(F32)
            bit *= 2
        if mask:
            z_send[mask] = summed.astype(BF16)
            z_copies[mask] = send(z_send.at[mask], z_recv.at[mask], flip(d, 4 * bit), f)
        else:
            grad_ref[...] = summed

    for place, mask in enumerate(masks):
        reduce_half(2 * place)
        if place:
            forward_block(masks[place - 1])
        reduce_half(2 * place + 1)
    forward_block(0)
    for copy in started:
        copy.wait_send()


def body(nd, nf, context, residual, weight, gain, pattern, positive):
    tokens, width = context.shape
    depth = weight.shape[0]
    seqs = positive.shape[0]
    nz = nd // 4
    bw = width // nd
    fold = width * 2 * seqs // 16
    lanes = 128
    vmem = pl.BlockSpec(memory_space=pltpu.VMEM)
    smem = pl.BlockSpec(memory_space=pltpu.SMEM)
    hbm = pl.BlockSpec(memory_space=pl.ANY)
    copies = count_copies(nd, nf)
    return pl.pallas_call(
        functools.partial(kernel, nd, nf, seqs),
        out_shape=(
            jax.ShapeDtypeStruct((seqs,), F32),
            jax.ShapeDtypeStruct((depth, bw), F32),
        ),
        in_specs=[hbm] * 5 + [smem],
        out_specs=(smem, vmem),
        scratch_shapes=[
            pltpu.VMEM((tokens, width), BF16),
            pltpu.VMEM((tokens, width), BF16),
            pltpu.VMEM((width,), BF16),
            pltpu.VMEM((1, nd), jnp.int32),
            pltpu.VMEM((nf, depth, width), BF16),
            pltpu.VMEM((tokens, width), F32),
            pltpu.VMEM((tokens, 128), F32),
            pltpu.VMEM((tokens, 128), F32),
            pltpu.VMEM((8, width), F32),
            pltpu.VMEM((nf, depth, tokens), BF16),
            pltpu.VMEM((2, nf, depth, tokens), BF16),
            pltpu.VMEM((16, lanes), BF16),
            pltpu.VMEM((nd, 16, lanes), BF16),
            pltpu.VMEM((16, fold), BF16),
            pltpu.VMEM((nd, 16, fold), BF16),
            pltpu.VMEM((2, nz, 2, tokens, bw), BF16),
            pltpu.VMEM((2, nf, nz, 2, tokens, bw), BF16),
            pltpu.VMEM((nz, depth, bw), BF16),
            pltpu.VMEM((nz, depth, bw), BF16),
            pltpu.VMEM((nz, depth, bw), F32),
            pltpu.VMEM((nz, depth, bw), BF16),
            pltpu.VMEM((nz, depth, bw), BF16),
            pltpu.SemaphoreType.DMA((5,)),
            pltpu.SemaphoreType.DMA((copies,)),
            pltpu.SemaphoreType.DMA((copies,)),
        ],
        compiler_params=pltpu.CompilerParams(
            collective_id=0, has_side_effects=True, vmem_limit_bytes=63 * 1024 * 1024
        ),
        cost_estimate=pl.CostEstimate(
            flops=8 * tokens * width * width, bytes_accessed=8 * depth * width, transcendentals=0
        ),
    )(context, residual, weight, gain, pattern, positive)


def solution(mesh):
    return jax.shard_map(
        functools.partial(body, mesh.shape["dp"], mesh.shape["fsdp"]),
        mesh=mesh,
        in_specs=(
            P(("dp", "fsdp"), None),
            P(("dp", "fsdp"), None),
            P("fsdp", None),
            P(),
            P(("dp", "fsdp"), None),
            P(("dp", "fsdp")),
        ),
        out_specs=(P(("dp", "fsdp")), P("fsdp", "dp")),
        check_vma=False,
    )
```

```python
import functools

import jax
import jax.numpy as jnp
from jax import lax
from jax.experimental import pallas as pl
from jax.experimental.pallas import tpu as pltpu
from jax.sharding import PartitionSpec as P

MESH = pl.DeviceIdType.MESH
F32 = jnp.float32
BF16 = jnp.bfloat16
NT = (((1,), (1,)), ((), ()))


def flip(index, mask):
    out = index
    bit = 1
    while bit <= mask:
        if mask & bit:
            out = out + bit * (1 - 2 * lax.rem(lax.div(index, bit), 2))
        bit *= 2
    return out


def count_copies(nd, nf):
    nz = nd // 4
    groups = nd // 2
    weights = (nf - 1) * 8 * 8
    return weights + 16 * (nf - 1) + 1 + 4 * groups + (2 * nf - 1) * 2 * nz + nz + nz - 1


def kernel(
    nd,
    nf,
    seqs,
    context_hbm,
    residual_hbm,
    weight_hbm,
    gain_hbm,
    pattern_hbm,
    positive_ref,
    loss_ref,
    grad_ref,
    ctx,
    res,
    gain_ref,
    pattern_ref,
    wg,
    hid,
    invs,
    slopes,
    g_rows,
    ctx_t,
    ctx_all,
    note,
    notes,
    msg,
    pool,
    dhs,
    dh_all,
    y_send,
    y_recv,
    kept,
    z_send,
    z_recv,
    local_sem,
    send_sem,
    recv_sem,
):
    d = lax.axis_index("dp")
    f = lax.axis_index("fsdp")
    tokens, width = ctx.shape
    depth = wg.shape[1]
    nz = nd // 4
    bw = width // nd
    core = lax.rem(d, 2)
    y = lax.rem(lax.div(d, 2), 2)
    z = lax.div(d, 4)
    spot = lax.rem(d, 8)
    length = tokens // (2 * seqs)
    parts = 8
    rows_in = depth // 8
    wide = width // parts
    other = lambda k: lax.rem(f + k, nf)
    source = lambda k: lax.rem(f + nf - k, nf)
    others = range(1, nf)

    started = []

    def send(src, dst, dd, ff):
        slot = len(started)
        copy = pltpu.make_async_remote_copy(
            src_ref=src,
            dst_ref=dst,
            send_sem=send_sem.at[slot],
            recv_sem=recv_sem.at[slot],
            device_id=(dd, ff),
            device_id_type=MESH,
        )
        copy.start()
        started.append(copy)
        return copy

    def load(src, dst, slot):
        copy = pltpu.make_async_copy(src, dst, local_sem.at[slot])
        copy.start()
        return copy

    loads = [
        load(context_hbm, ctx, 0),
        load(weight_hbm, wg.at[f], 1),
        load(residual_hbm, res, 2),
        load(gain_hbm, gain_ref, 3),
        load(pattern_hbm, pattern_ref, 4),
    ]

    barrier = pltpu.get_barrier_semaphore()
    sibling = flip(d, 1)
    partners = [(lax.rem(d + 2 * s, nd), f) for s in range(1, nd // 2)] + [(sibling, f)]
    partners += [(d, other(k)) for k in others] + [(sibling, other(k)) for k in others]
    for partner in partners:
        pl.semaphore_signal(barrier, inc=1, device_id=partner, device_id_type=MESH)
    pl.semaphore_wait(barrier, len(partners))

    near_y, near_z, far = flip(spot, 2), flip(spot, 4), flip(spot, 6)

    def piece(place, h):
        return (pl.ds(pl.multiple_of(place * rows_in, rows_in), rows_in), slice(h * wide, (h + 1) * wide))

    def fetch(place, h):
        at = piece(place, h)
        return [send(weight_hbm.at[at], wg.at[(f, *at)], d, other(k)) for k in others]

    def pass_on(place, h, mask):
        at = piece(place, h)
        copies = []
        for k in others:
            ref = wg.at[(source(k), *at)]
            copies.append(send(ref, ref, flip(d, mask), f))
        return copies

    def arrive(copies):
        for copy in copies:
            copy.wait_recv()

    direct = {0: fetch(spot, 0)}

    loads[4].wait()
    lanes = note.shape[1]
    lane_id = lax.broadcasted_iota(jnp.int32, (16, lanes), 1)
    row_id = lax.broadcasted_iota(jnp.int32, (16, lanes), 0)
    log_s = seqs.bit_length() - 1
    spread_lane = lax.broadcasted_iota(jnp.int32, (nd, lanes), 1) >> log_s
    spread = spread_lane == lax.broadcasted_iota(jnp.int32, (nd, lanes), 0)
    pattern = jnp.broadcast_to(pattern_ref[...].astype(F32), (16, nd)).astype(BF16)
    allowed_row = jnp.dot(
        pattern, jnp.where(spread, 1.0, 0.0).astype(BF16), preferred_element_type=F32
    )
    meta = jnp.where(row_id < seqs, allowed_row, 0.0)
    for s in range(seqs):
        hit = jnp.logical_and(row_id == seqs + s, lane_id == positive_ref[s] + d * seqs)
        meta = jnp.where(hit, 1.0, meta)
    note[...] = meta.astype(BF16)
    notes[d] = note[...]
    near = [lax.rem(d + 2 * s, nd) for s in range(nd // 2 - 1, 0, -1)]
    behind = [lax.rem(d + nd - 2 * s, nd) for s in range(nd // 2 - 1, 0, -1)]
    note_copies = [send(note, notes.at[d], there, f) for there in near]
    note_pairs = [send(note, notes.at[d], sibling, f)]

    loads[0].wait()
    for part in range(nf):
        ctx_t[part] = ctx[:, part * depth : (part + 1) * depth].T
    direct[1] = fetch(spot, 1)
    ctx_all[core, f] = ctx_t[f]
    sibling_ctx = [send(ctx_all.at[core, f], ctx_all.at[core, f], sibling, f)]
    loads[1].wait()
    loads[2].wait()
    tile = 256

    def project(shard, first, start, count):
        def step(n, carry):
            cols = pl.ds(pl.multiple_of(n * tile, tile), tile)
            left = ctx[:, pl.ds(pl.multiple_of(shard * depth, 128), depth)]
            before = res[:, cols].astype(F32) if first else hid[:, cols]
            hid[:, cols] = before + jnp.dot(left, wg[shard, :, cols], preferred_element_type=F32)
            return carry

        lax.fori_loop(start // tile, (start + count) // tile, step, 0)

    to_y, to_z, to_core, to_far = {}, {}, {h: [] for h in range(parts)}, {}
    chunks = 8
    ctx_copies = {}

    def chunk(i):
        return slice(i * depth // chunks, (i + 1) * depth // chunks)

    def trickle(i):
        for k in others:
            src, dst = ctx_t.at[other(k), chunk(i)], ctx_all.at[core, f, chunk(i)]
            ctx_copies[i, k] = send(src, dst, d, other(k))

    def relay(i):
        for k in others:
            ctx_copies[i, k].wait_recv()
            ref = ctx_all.at[core, source(k), chunk(i)]
            sibling_ctx.append(send(ref, ref, sibling, f))

    by_y, by_z = range(0, parts // 4), range(parts // 4, parts // 2)

    def from_x(h):
        arrive(direct[h])
        to_y[h] = pass_on(spot, h, 2)
        to_z[h] = pass_on(spot, h, 4)
        to_core[h] += pass_on(spot, h, 1)
        if h + 2 < parts:
            direct[h + 2] = fetch(spot, h + 2)
            if h + 2 >= parts // 2:
                to_far[h + 2] = fetch(far, h + 2)

    def from_near(h):
        for copies, place, turn, routed in (
            (to_z[h], near_z, 2, by_y),
            (to_y[h], near_y, 4, by_z),
        ):
            arrive(copies)
            if h in routed:
                to_far[h] = pass_on(place, h, turn)
            to_core[h] += pass_on(place, h, 1)

    def from_far(h):
        arrive(to_far[h])
        to_core[h] += pass_on(far, h, 1)

    def finish(h):
        arrive(to_core[h])
        for k in others:
            project(source(k), False, h * wide, wide)

    for t in range(parts + 3):
        if t < parts:
            from_x(t)
        if t == 0:
            project(f, True, 0, width)
        if 0 <= t - 1 < parts:
            from_near(t - 1)
        if 0 <= t - 2 < parts:
            from_far(t - 2)
        if t >= parts - 1:
            trickle(t - parts + 1)
        if t == parts:
            for copy, origin in zip(note_copies, behind):
                copy.wait_recv()
                note_pairs.append(send(notes.at[origin], notes.at[origin], sibling, f))
        if t >= 3:
            finish(t - 3)

    loads[3].wait()
    gain = gain_ref[...].astype(F32).reshape(1, width)
    pooled_rows = []
    for s in range(2 * seqs):
        rows = slice(s * length, (s + 1) * length)
        h_rows = hid[rows, :]
        inv = lax.rsqrt(jnp.mean(h_rows * h_rows, axis=1, keepdims=True) + 1e-05)
        invs[rows, :] = jnp.broadcast_to(inv, (length, invs.shape[1]))
        pooled_rows.append(jnp.sum(h_rows * inv, axis=0, keepdims=True))
    pooled = jnp.concatenate(pooled_rows, axis=0) * (gain / length)
    scale = lax.rsqrt(jnp.sum(pooled * pooled, axis=1, keepdims=True) + 1e-06)
    unit = pooled * scale
    per = 2 * seqs
    folds = 16 // per
    fold = width // folds
    folded = jnp.concatenate([unit[:, i * fold : (i + 1) * fold] for i in range(folds)], axis=0)
    msg[...] = folded.astype(BF16)
    pool_copies = [send(msg, pool.at[d], there, f) for there in near]
    pool_pairs = [send(msg, pool.at[d], sibling, f)]
    pool[d] = msg[...]

    cols = nd * seqs
    total_rows = nd * 16
    log_p = per.bit_length() - 1
    flat = lax.broadcasted_iota(jnp.int32, (cols, total_rows), 1)
    col = lax.broadcasted_iota(jnp.int32, (cols, total_rows), 0)
    owner = (flat >> 4) == (col >> log_s)
    inner, slot_in = flat & (per - 1), col & (seqs - 1)
    pick_q = jnp.where(jnp.logical_and(owner, inner == slot_in), 1.0, 0.0).astype(BF16)
    pick_p = jnp.where(jnp.logical_and(owner, inner == slot_in + seqs), 1.0, 0.0).astype(BF16)
    row_fold = (lax.broadcasted_iota(jnp.int32, (total_rows, total_rows), 0) & 15) >> log_p
    col_fold = (lax.broadcasted_iota(jnp.int32, (total_rows, total_rows), 1) & 15) >> log_p
    same = jnp.where(row_fold == col_fold, 1.0, 0.0)
    lane_col = lax.broadcasted_iota(jnp.int32, (16, cols), 1) - d * seqs
    row_in = lax.broadcasted_iota(jnp.int32, (16, cols), 0) & (per - 1)
    hit_q = jnp.logical_and(lane_col == row_in, row_in < seqs)
    hit_p = jnp.logical_and(lane_col + seqs == row_in, row_in >= seqs)
    mine_q = jnp.where(hit_q, 1.0, 0.0).astype(BF16)
    mine_p = jnp.where(hit_p, 1.0, 0.0).astype(BF16)
    arrive(note_pairs)
    info = notes[...].reshape(total_rows, lanes)
    allowed = jnp.dot(pick_q, info, preferred_element_type=F32)[:, :cols]
    onehot = jnp.dot(pick_p, info, preferred_element_type=F32)[:, :cols]

    for copy, origin in zip(pool_copies, behind):
        copy.wait_recv()
        pool_pairs.append(send(pool.at[origin], pool.at[origin], sibling, f))
    for i in range(4, 8):
        trickle(i)
    for i in range(4):
        relay(i)
    arrive(pool_pairs)

    def three(value):
        high = value.astype(BF16)
        rest = value - high.astype(F32)
        middle = rest.astype(BF16)
        return high, middle, (rest - middle.astype(F32)).astype(BF16)

    x = pool[...].reshape(total_rows, fold)
    gram = lax.dot_general(x, x, NT, preferred_element_type=F32) * same
    half = sum(jnp.dot(pick_q, part, preferred_element_type=F32) for part in three(gram))
    scores = 20.0 * sum(
        lax.dot_general(part, pick_p, NT, preferred_element_type=F32) for part in three(half)
    )
    weighted = allowed * jnp.exp(scores)
    total = jnp.sum(weighted, axis=1, keepdims=True)
    losses = jnp.log(total) - jnp.sum(onehot * scores, axis=1, keepdims=True)
    coeff = (weighted / total - onehot).astype(BF16)
    coeff_q = jnp.dot(mine_q, coeff, preferred_element_type=F32).astype(BF16)
    coeff_p = lax.dot_general(mine_p, coeff, NT, preferred_element_type=F32).astype(BF16)
    mix = jnp.dot(coeff_q, pick_p, preferred_element_type=F32)
    mix = mix + jnp.dot(coeff_p, pick_q, preferred_element_type=F32)
    mix = (mix * same[:16, :]).astype(BF16)
    d_fold = 20.0 * jnp.dot(mix, x, preferred_element_type=F32)
    d_embed = jnp.concatenate([d_fold[i * per : (i + 1) * per, :] for i in range(folds)], axis=1)
    d_pooled = (d_embed - unit * jnp.sum(unit * d_embed, axis=1, keepdims=True)) * scale
    d_gated = d_pooled * (gain / length)

    g_rows[0:per, :] = d_gated
    for s in range(per):
        rows = slice(s * length, (s + 1) * length)
        inv = invs[rows, 0:1]
        mean = jnp.mean(hid[rows, :] * d_gated[s : s + 1, :], axis=1, keepdims=True)
        slopes[rows, :] = jnp.broadcast_to(inv * inv * inv * mean, (length, slopes.shape[1]))

    def differentiate(block):
        at = pl.ds(pl.multiple_of(block * 4 * bw, 128), 4 * bw)
        for s in range(per):
            rows = slice(s * length, (s + 1) * length)
            inv, slope = invs[rows, 0:1], slopes[rows, 0:1]
            d_rows = inv * g_rows[s : s + 1, at] - hid[rows, at] * slope
            for j in range(4):
                dhs[j % 2, block, j // 2, rows, :] = d_rows[:, j * bw : (j + 1) * bw].astype(BF16)

    masks = list(range(nz - 1, -1, -1))
    peers = [(dc, k) for dc in range(2) for k in range(nf) if (dc, k) != (0, 0)]
    dh_copies = {}
    halves = [(masks[0], 1)]
    for ahead, mask in zip(masks[1:], masks):
        halves += [(ahead, 1), (mask, 0)]
    halves.append((masks[-1], 0))

    def share(mask, away):
        block, side = flip(z, mask), flip(y, away)
        for dc, k in peers:
            dh_copies[mask, away, dc, k] = send(
                dhs.at[flip(core, dc), block, side],
                dh_all.at[core, f, block, side],
                flip(d, dc),
                other(k),
            )

    for place, mask in enumerate(masks):
        differentiate(flip(z, mask))
        if place < 2:
            share(*halves[place])
    for i in range(4, 8):
        relay(i)
    col_id = lax.broadcasted_iota(jnp.int32, (cols, 1), 0)
    for s in range(seqs):
        loss_ref[s] = jnp.sum(jnp.where(col_id == d * seqs + s, losses, 0.0))
    arrive(sibling_ctx)

    row_tile = min(256, depth)
    y_copies, z_copies = {}, {}

    def reduce_half(place):
        mask, away = halves[place]
        block, side = flip(z, mask), flip(y, away)
        for dc, k in peers:
            dh_copies[mask, away, dc, k].wait_recv()
        if place + 2 < len(halves):
            share(*halves[place + 2])

        def step(n, carry):
            at = pl.ds(pl.multiple_of(n * row_tile, row_tile), row_tile)
            total = jnp.dot(
                ctx_all[core, f, at, :], dhs[core, block, side], preferred_element_type=F32
            )
            for dc, k in peers:
                a, b = flip(core, dc), source(k)
                total += jnp.dot(
                    ctx_all[a, b, at, :], dh_all[a, b, block, side], preferred_element_type=F32
                )
            if away:
                y_send[mask, at, :] = total.astype(BF16)
            else:
                kept[mask, at, :] = total
            return carry

        lax.fori_loop(0, depth // row_tile, step, 0)
        if away:
            y_copies[mask] = send(y_send.at[mask], y_recv.at[mask], flip(d, 2), f)

    def forward_block(mask):
        y_copies[mask].wait_recv()
        summed = kept[mask] + y_recv[mask].astype(F32)
        bit = 1
        while bit < nz and not mask & bit:
            z_copies[mask | bit].wait_recv()
            summed = summed + z_recv[mask | bit].astype(F32)
            bit *= 2
        if mask:
            z_send[mask] = summed.astype(BF16)
            z_copies[mask] = send(z_send.at[mask], z_recv.at[mask], flip(d, 4 * bit), f)
        else:
            grad_ref[...] = summed

    for place, (mask, away) in enumerate(halves):
        reduce_half(place)
        if not away:
            forward_block(mask)
    for copy in started:
        copy.wait_send()


def body(nd, nf, context, residual, weight, gain, pattern, positive):
    tokens, width = context.shape
    depth = weight.shape[0]
    seqs = positive.shape[0]
    nz = nd // 4
    bw = width // nd
    fold = width * 2 * seqs // 16
    lanes = 128
    vmem = pl.BlockSpec(memory_space=pltpu.VMEM)
    smem = pl.BlockSpec(memory_space=pltpu.SMEM)
    hbm = pl.BlockSpec(memory_space=pl.ANY)
    copies = count_copies(nd, nf)
    return pl.pallas_call(
        functools.partial(kernel, nd, nf, seqs),
        out_shape=(
            jax.ShapeDtypeStruct((seqs,), F32),
            jax.ShapeDtypeStruct((depth, bw), F32),
        ),
        in_specs=[hbm] * 5 + [smem],
        out_specs=(smem, vmem),
        scratch_shapes=[
            pltpu.VMEM((tokens, width), BF16),
            pltpu.VMEM((tokens, width), BF16),
            pltpu.VMEM((width,), BF16),
            pltpu.VMEM((1, nd), jnp.int32),
            pltpu.VMEM((nf, depth, width), BF16),
            pltpu.VMEM((tokens, width), F32),
            pltpu.VMEM((tokens, 128), F32),
            pltpu.VMEM((tokens, 128), F32),
            pltpu.VMEM((8, width), F32),
            pltpu.VMEM((nf, depth, tokens), BF16),
            pltpu.VMEM((2, nf, depth, tokens), BF16),
            pltpu.VMEM((16, lanes), BF16),
            pltpu.VMEM((nd, 16, lanes), BF16),
            pltpu.VMEM((16, fold), BF16),
            pltpu.VMEM((nd, 16, fold), BF16),
            pltpu.VMEM((2, nz, 2, tokens, bw), BF16),
            pltpu.VMEM((2, nf, nz, 2, tokens, bw), BF16),
            pltpu.VMEM((nz, depth, bw), BF16),
            pltpu.VMEM((nz, depth, bw), BF16),
            pltpu.VMEM((nz, depth, bw), F32),
            pltpu.VMEM((nz, depth, bw), BF16),
            pltpu.VMEM((nz, depth, bw), BF16),
            pltpu.SemaphoreType.DMA((5,)),
            pltpu.SemaphoreType.DMA((copies,)),
            pltpu.SemaphoreType.DMA((copies,)),
        ],
        compiler_params=pltpu.CompilerParams(
            collective_id=0, has_side_effects=True, vmem_limit_bytes=63 * 1024 * 1024
        ),
        cost_estimate=pl.CostEstimate(
            flops=8 * tokens * width * width, bytes_accessed=8 * depth * width, transcendentals=0
        ),
    )(context, residual, weight, gain, pattern, positive)


def solution(mesh):
    return jax.shard_map(
        functools.partial(body, mesh.shape["dp"], mesh.shape["fsdp"]),
        mesh=mesh,
        in_specs=(
            P(("dp", "fsdp"), None),
            P(("dp", "fsdp"), None),
            P("fsdp", None),
            P(),
            P(("dp", "fsdp"), None),
            P(("dp", "fsdp")),
        ),
        out_specs=(P(("dp", "fsdp")), P("fsdp", "dp")),
        check_vma=False,
    )
```

```python
import functools

import jax
import jax.numpy as jnp
from jax import lax
from jax.experimental import pallas as pl
from jax.experimental.pallas import tpu as pltpu
from jax.sharding import PartitionSpec as P

MESH = pl.DeviceIdType.MESH
F32 = jnp.float32
BF16 = jnp.bfloat16
NT = (((1,), (1,)), ((), ()))


def flip(index, mask):
    out = index
    bit = 1
    while bit <= mask:
        if mask & bit:
            out = out + bit * (1 - 2 * lax.rem(lax.div(index, bit), 2))
        bit *= 2
    return out


def count_copies(nd, nf):
    nz = nd // 4
    groups = nd // 2
    weights = (nf - 1) * (4 + 2 + 5 + 5 + 16)
    return weights + 16 * (nf - 1) + 1 + 4 * groups + (2 * nf - 1) * 2 * nz + nz + nz - 1


def kernel(
    nd,
    nf,
    seqs,
    context_hbm,
    residual_hbm,
    weight_hbm,
    gain_hbm,
    pattern_hbm,
    positive_ref,
    loss_ref,
    grad_ref,
    ctx,
    res,
    gain_ref,
    pattern_ref,
    wg,
    hid,
    invs,
    slopes,
    g_rows,
    ctx_t,
    ctx_all,
    note,
    notes,
    msg,
    pool,
    dhs,
    dh_all,
    y_send,
    y_recv,
    kept,
    z_send,
    z_recv,
    local_sem,
    send_sem,
    recv_sem,
):
    d = lax.axis_index("dp")
    f = lax.axis_index("fsdp")
    tokens, width = ctx.shape
    depth = wg.shape[1]
    nz = nd // 4
    bw = width // nd
    core = lax.rem(d, 2)
    y = lax.rem(lax.div(d, 2), 2)
    z = lax.div(d, 4)
    spot = lax.rem(d, 8)
    length = tokens // (2 * seqs)
    parts = 4
    rows_in = depth // 8
    wide = width // parts
    other = lambda k: lax.rem(f + k, nf)
    source = lambda k: lax.rem(f + nf - k, nf)
    others = range(1, nf)

    started = []

    def send(src, dst, dd, ff):
        slot = len(started)
        copy = pltpu.make_async_remote_copy(
            src_ref=src,
            dst_ref=dst,
            send_sem=send_sem.at[slot],
            recv_sem=recv_sem.at[slot],
            device_id=(dd, ff),
            device_id_type=MESH,
        )
        copy.start()
        started.append(copy)
        return copy

    def load(src, dst, slot):
        copy = pltpu.make_async_copy(src, dst, local_sem.at[slot])
        copy.start()
        return copy

    loads = [
        load(context_hbm, ctx, 0),
        load(weight_hbm, wg.at[f], 1),
        load(residual_hbm, res, 2),
        load(gain_hbm, gain_ref, 3),
        load(pattern_hbm, pattern_ref, 4),
    ]

    barrier = pltpu.get_barrier_semaphore()
    sibling = flip(d, 1)
    partners = [(lax.rem(d + 2 * s, nd), f) for s in range(1, nd // 2)] + [(sibling, f)]
    partners += [(d, other(k)) for k in others] + [(sibling, other(k)) for k in others]
    for partner in partners:
        pl.semaphore_signal(barrier, inc=1, device_id=partner, device_id_type=MESH)
    pl.semaphore_wait(barrier, len(partners))

    near_y, near_z, far = flip(spot, 2), flip(spot, 4), flip(spot, 6)

    def piece(place, h):
        return (pl.ds(pl.multiple_of(place * rows_in, rows_in), rows_in), slice(h * wide, (h + 1) * wide))

    def fetch(place, h):
        at = piece(place, h)
        return [send(weight_hbm.at[at], wg.at[(f, *at)], d, other(k)) for k in others]

    def pass_on(place, h, mask):
        at = piece(place, h)
        copies = []
        for k in others:
            ref = wg.at[(source(k), *at)]
            copies.append(send(ref, ref, flip(d, mask), f))
        return copies

    def arrive(copies):
        for copy in copies:
            copy.wait_recv()

    direct = {0: fetch(spot, 0)}

    loads[4].wait()
    lanes = note.shape[1]
    lane_id = lax.broadcasted_iota(jnp.int32, (16, lanes), 1)
    row_id = lax.broadcasted_iota(jnp.int32, (16, lanes), 0)
    log_s = seqs.bit_length() - 1
    spread_lane = lax.broadcasted_iota(jnp.int32, (nd, lanes), 1) >> log_s
    spread = spread_lane == lax.broadcasted_iota(jnp.int32, (nd, lanes), 0)
    pattern = jnp.broadcast_to(pattern_ref[...].astype(F32), (16, nd)).astype(BF16)
    allowed_row = jnp.dot(
        pattern, jnp.where(spread, 1.0, 0.0).astype(BF16), preferred_element_type=F32
    )
    meta = jnp.where(row_id < seqs, allowed_row, 0.0)
    for s in range(seqs):
        hit = jnp.logical_and(row_id == seqs + s, lane_id == positive_ref[s] + d * seqs)
        meta = jnp.where(hit, 1.0, meta)
    note[...] = meta.astype(BF16)
    notes[d] = note[...]
    near = [lax.rem(d + 2 * s, nd) for s in range(1, nd // 2)]
    behind = [lax.rem(d + nd - 2 * s, nd) for s in range(1, nd // 2)]
    note_copies = [send(note, notes.at[d], there, f) for there in near]
    note_pairs = [send(note, notes.at[d], sibling, f)]

    loads[0].wait()
    for part in range(nf):
        ctx_t[part] = ctx[:, part * depth : (part + 1) * depth].T
    direct[1] = fetch(spot, 1)
    ctx_all[core, f] = ctx_t[f]
    sibling_ctx = [send(ctx_all.at[core, f], ctx_all.at[core, f], sibling, f)]
    loads[1].wait()
    loads[2].wait()
    tile = 256

    def project(shard, first, start, count):
        def step(n, carry):
            cols = pl.ds(pl.multiple_of(n * tile, tile), tile)
            left = ctx[:, pl.ds(pl.multiple_of(shard * depth, 128), depth)]
            before = res[:, cols].astype(F32) if first else hid[:, cols]
            hid[:, cols] = before + jnp.dot(left, wg[shard, :, cols], preferred_element_type=F32)
            return carry

        lax.fori_loop(start // tile, (start + count) // tile, step, 0)

    arrive(direct[0])
    to_y, to_z, to_core, straight = {}, {}, {h: [] for h in range(parts)}, {}

    def spread_out(h):
        to_y[h] = pass_on(spot, h, 2)
        to_z[h] = pass_on(spot, h, 4)
        to_core[h] += pass_on(spot, h, 1)

    def finish(h):
        arrive(to_core[h])
        for k in others:
            project(source(k), False, h * wide, wide)

    chunks = 1
    ctx_copies = {}

    def chunk(i):
        return slice(i * depth // chunks, (i + 1) * depth // chunks)

    def trickle(i):
        for k in others:
            src, dst = ctx_t.at[other(k), chunk(i)], ctx_all.at[core, f, chunk(i)]
            ctx_copies[i, k] = send(src, dst, d, other(k))

    def relay(i):
        for k in others:
            ctx_copies[i, k].wait_recv()
            ref = ctx_all.at[core, source(k), chunk(i)]
            sibling_ctx.append(send(ref, ref, sibling, f))

    spread_out(0)
    direct[2], straight[2] = fetch(spot, 2), fetch(far, 2)
    project(f, True, 0, width)
    arrive(direct[1])
    spread_out(1)
    direct[3], straight[3] = fetch(spot, 3), fetch(far, 3)
    arrive(to_z[0])
    across_y = pass_on(near_z, 0, 2)
    to_core[0] += pass_on(near_z, 0, 1)
    arrive(to_y[0])
    to_core[0] += pass_on(near_y, 0, 1)
    arrive(direct[2])
    spread_out(2)
    arrive(to_y[1])
    across_z = pass_on(near_y, 1, 4)
    to_core[1] += pass_on(near_y, 1, 1)
    arrive(to_z[1])
    to_core[1] += pass_on(near_z, 1, 1)
    arrive(straight[2])
    to_core[2] += pass_on(far, 2, 1)
    arrive(across_y)
    to_core[0] += pass_on(far, 0, 1)
    arrive(direct[3])
    spread_out(3)
    trickle(0)
    finish(0)
    arrive(across_z)
    to_core[1] += pass_on(far, 1, 1)
    arrive(to_y[2])
    to_core[2] += pass_on(near_y, 2, 1)
    arrive(to_z[2])
    to_core[2] += pass_on(near_z, 2, 1)
    arrive(straight[3])
    to_core[3] += pass_on(far, 3, 1)
    finish(1)
    finish(2)
    arrive(to_y[3])
    to_core[3] += pass_on(near_y, 3, 1)
    arrive(to_z[3])
    to_core[3] += pass_on(near_z, 3, 1)
    for copy, origin in zip(note_copies, behind):
        copy.wait_recv()
        note_pairs.append(send(notes.at[origin], notes.at[origin], sibling, f))
    finish(3)

    loads[3].wait()
    gain = gain_ref[...].astype(F32).reshape(1, width)
    pooled_rows = []
    for s in range(2 * seqs):
        rows = slice(s * length, (s + 1) * length)
        h_rows = hid[rows, :]
        inv = lax.rsqrt(jnp.mean(h_rows * h_rows, axis=1, keepdims=True) + 1e-05)
        invs[rows, :] = jnp.broadcast_to(inv, (length, invs.shape[1]))
        pooled_rows.append(jnp.sum(h_rows * inv, axis=0, keepdims=True))
    pooled = jnp.concatenate(pooled_rows, axis=0) * (gain / length)
    scale = lax.rsqrt(jnp.sum(pooled * pooled, axis=1, keepdims=True) + 1e-06)
    unit = pooled * scale
    per = 2 * seqs
    folds = 16 // per
    fold = width // folds
    folded = jnp.concatenate([unit[:, i * fold : (i + 1) * fold] for i in range(folds)], axis=0)
    msg[...] = folded.astype(BF16)
    pool_copies = [send(msg, pool.at[d], there, f) for there in near]
    pool_pairs = [send(msg, pool.at[d], sibling, f)]
    pool[d] = msg[...]

    cols = nd * seqs
    total_rows = nd * 16
    log_p = per.bit_length() - 1
    flat = lax.broadcasted_iota(jnp.int32, (cols, total_rows), 1)
    col = lax.broadcasted_iota(jnp.int32, (cols, total_rows), 0)
    owner = (flat >> 4) == (col >> log_s)
    inner, slot_in = flat & (per - 1), col & (seqs - 1)
    pick_q = jnp.where(jnp.logical_and(owner, inner == slot_in), 1.0, 0.0).astype(BF16)
    pick_p = jnp.where(jnp.logical_and(owner, inner == slot_in + seqs), 1.0, 0.0).astype(BF16)
    row_fold = (lax.broadcasted_iota(jnp.int32, (total_rows, total_rows), 0) & 15) >> log_p
    col_fold = (lax.broadcasted_iota(jnp.int32, (total_rows, total_rows), 1) & 15) >> log_p
    same = jnp.where(row_fold == col_fold, 1.0, 0.0)
    lane_col = lax.broadcasted_iota(jnp.int32, (16, cols), 1) - d * seqs
    row_in = lax.broadcasted_iota(jnp.int32, (16, cols), 0) & (per - 1)
    hit_q = jnp.logical_and(lane_col == row_in, row_in < seqs)
    hit_p = jnp.logical_and(lane_col + seqs == row_in, row_in >= seqs)
    mine_q = jnp.where(hit_q, 1.0, 0.0).astype(BF16)
    mine_p = jnp.where(hit_p, 1.0, 0.0).astype(BF16)
    arrive(note_pairs)
    info = notes[...].reshape(total_rows, lanes)
    allowed = jnp.dot(pick_q, info, preferred_element_type=F32)[:, :cols]
    onehot = jnp.dot(pick_p, info, preferred_element_type=F32)[:, :cols]

    for copy, origin in zip(pool_copies, behind):
        copy.wait_recv()
        pool_pairs.append(send(pool.at[origin], pool.at[origin], sibling, f))
    relay(0)
    arrive(pool_pairs)

    def three(value):
        high = value.astype(BF16)
        rest = value - high.astype(F32)
        middle = rest.astype(BF16)
        return high, middle, (rest - middle.astype(F32)).astype(BF16)

    x = pool[...].reshape(total_rows, fold)
    gram = lax.dot_general(x, x, NT, preferred_element_type=F32) * same
    half = sum(jnp.dot(pick_q, part, preferred_element_type=F32) for part in three(gram))
    scores = 20.0 * sum(
        lax.dot_general(part, pick_p, NT, preferred_element_type=F32) for part in three(half)
    )
    weighted = allowed * jnp.exp(scores)
    total = jnp.sum(weighted, axis=1, keepdims=True)
    losses = jnp.log(total) - jnp.sum(onehot * scores, axis=1, keepdims=True)
    coeff = (weighted / total - onehot).astype(BF16)
    coeff_q = jnp.dot(mine_q, coeff, preferred_element_type=F32).astype(BF16)
    coeff_p = lax.dot_general(mine_p, coeff, NT, preferred_element_type=F32).astype(BF16)
    mix = jnp.dot(coeff_q, pick_p, preferred_element_type=F32)
    mix = mix + jnp.dot(coeff_p, pick_q, preferred_element_type=F32)
    mix = (mix * same[:16, :]).astype(BF16)
    d_fold = 20.0 * jnp.dot(mix, x, preferred_element_type=F32)
    d_embed = jnp.concatenate([d_fold[i * per : (i + 1) * per, :] for i in range(folds)], axis=1)
    d_pooled = (d_embed - unit * jnp.sum(unit * d_embed, axis=1, keepdims=True)) * scale
    d_gated = d_pooled * (gain / length)

    g_rows[0:per, :] = d_gated
    for s in range(per):
        rows = slice(s * length, (s + 1) * length)
        inv = invs[rows, 0:1]
        mean = jnp.mean(hid[rows, :] * d_gated[s : s + 1, :], axis=1, keepdims=True)
        slopes[rows, :] = jnp.broadcast_to(inv * inv * inv * mean, (length, slopes.shape[1]))

    def differentiate(block):
        at = pl.ds(pl.multiple_of(block * 4 * bw, 128), 4 * bw)
        for s in range(per):
            rows = slice(s * length, (s + 1) * length)
            inv, slope = invs[rows, 0:1], slopes[rows, 0:1]
            d_rows = inv * g_rows[s : s + 1, at] - hid[rows, at] * slope
            for j in range(4):
                dhs[j % 2, block, j // 2, rows, :] = d_rows[:, j * bw : (j + 1) * bw].astype(BF16)

    masks = list(range(nz - 1, -1, -1))
    peers = [(dc, k) for dc in range(2) for k in range(nf) if (dc, k) != (0, 0)]
    dh_copies = {}
    halves = [(masks[0], 1)]
    for ahead, mask in zip(masks[1:], masks):
        halves += [(ahead, 1), (mask, 0)]
    halves.append((masks[-1], 0))

    def share(mask, away):
        block, side = flip(z, mask), flip(y, away)
        for dc, k in peers:
            dh_copies[mask, away, dc, k] = send(
                dhs.at[flip(core, dc), block, side],
                dh_all.at[core, f, block, side],
                flip(d, dc),
                other(k),
            )

    for place, mask in enumerate(masks):
        differentiate(flip(z, mask))
        if place < 2:
            share(*halves[place])
    col_id = lax.broadcasted_iota(jnp.int32, (cols, 1), 0)
    for s in range(seqs):
        loss_ref[s] = jnp.sum(jnp.where(col_id == d * seqs + s, losses, 0.0))
    first_shared = len(started) - 2 * len(peers)
    for copy in started[:first_shared]:
        copy.wait_send()
    arrive(sibling_ctx)

    row_tile = min(256, depth)
    y_copies, z_copies = {}, {}

    def reduce_half(place):
        mask, away = halves[place]
        block, side = flip(z, mask), flip(y, away)
        for dc, k in peers:
            dh_copies[mask, away, dc, k].wait_recv()
        if place + 2 < len(halves):
            share(*halves[place + 2])

        def step(n, carry):
            at = pl.ds(pl.multiple_of(n * row_tile, row_tile), row_tile)
            total = jnp.dot(
                ctx_all[core, f, at, :], dhs[core, block, side], preferred_element_type=F32
            )
            for dc, k in peers:
                a, b = flip(core, dc), source(k)
                total += jnp.dot(
                    ctx_all[a, b, at, :], dh_all[a, b, block, side], preferred_element_type=F32
                )
            if away:
                y_send[mask, at, :] = total.astype(BF16)
            else:
                kept[mask, at, :] = total
            return carry

        lax.fori_loop(0, depth // row_tile, step, 0)
        if away:
            y_copies[mask] = send(y_send.at[mask], y_recv.at[mask], flip(d, 2), f)

    def forward_block(mask):
        y_copies[mask].wait_recv()
        summed = kept[mask] + y_recv[mask].astype(F32)
        bit = 1
        while bit < nz and not mask & bit:
            z_copies[mask | bit].wait_recv()
            summed = summed + z_recv[mask | bit].astype(F32)
            bit *= 2
        if mask:
            z_send[mask] = summed.astype(BF16)
            z_copies[mask] = send(z_send.at[mask], z_recv.at[mask], flip(d, 4 * bit), f)
        else:
            grad_ref[...] = summed

    for place, (mask, away) in enumerate(halves):
        reduce_half(place)
        if not away:
            forward_block(mask)
    for copy in started[first_shared:]:
        copy.wait_send()


def body(nd, nf, context, residual, weight, gain, pattern, positive):
    tokens, width = context.shape
    depth = weight.shape[0]
    seqs = positive.shape[0]
    nz = nd // 4
    bw = width // nd
    fold = width * 2 * seqs // 16
    lanes = 128
    vmem = pl.BlockSpec(memory_space=pltpu.VMEM)
    smem = pl.BlockSpec(memory_space=pltpu.SMEM)
    hbm = pl.BlockSpec(memory_space=pl.ANY)
    copies = count_copies(nd, nf)
    return pl.pallas_call(
        functools.partial(kernel, nd, nf, seqs),
        out_shape=(
            jax.ShapeDtypeStruct((seqs,), F32),
            jax.ShapeDtypeStruct((depth, bw), F32),
        ),
        in_specs=[hbm] * 5 + [smem],
        out_specs=(smem, vmem),
        scratch_shapes=[
            pltpu.VMEM((tokens, width), BF16),
            pltpu.VMEM((tokens, width), BF16),
            pltpu.VMEM((width,), BF16),
            pltpu.VMEM((1, nd), jnp.int32),
            pltpu.VMEM((nf, depth, width), BF16),
            pltpu.VMEM((tokens, width), F32),
            pltpu.VMEM((tokens, 128), F32),
            pltpu.VMEM((tokens, 128), F32),
            pltpu.VMEM((8, width), F32),
            pltpu.VMEM((nf, depth, tokens), BF16),
            pltpu.VMEM((2, nf, depth, tokens), BF16),
            pltpu.VMEM((16, lanes), BF16),
            pltpu.VMEM((nd, 16, lanes), BF16),
            pltpu.VMEM((16, fold), BF16),
            pltpu.VMEM((nd, 16, fold), BF16),
            pltpu.VMEM((2, nz, 2, tokens, bw), BF16),
            pltpu.VMEM((2, nf, nz, 2, tokens, bw), BF16),
            pltpu.VMEM((nz, depth, bw), BF16),
            pltpu.VMEM((nz, depth, bw), BF16),
            pltpu.VMEM((nz, depth, bw), F32),
            pltpu.VMEM((nz, depth, bw), BF16),
            pltpu.VMEM((nz, depth, bw), BF16),
            pltpu.SemaphoreType.DMA((5,)),
            pltpu.SemaphoreType.DMA((copies,)),
            pltpu.SemaphoreType.DMA((copies,)),
        ],
        compiler_params=pltpu.CompilerParams(
            collective_id=0, has_side_effects=True, vmem_limit_bytes=63 * 1024 * 1024
        ),
        cost_estimate=pl.CostEstimate(
            flops=8 * tokens * width * width, bytes_accessed=8 * depth * width, transcendentals=0
        ),
    )(context, residual, weight, gain, pattern, positive)


def solution(mesh):
    return jax.shard_map(
        functools.partial(body, mesh.shape["dp"], mesh.shape["fsdp"]),
        mesh=mesh,
        in_specs=(
            P(("dp", "fsdp"), None),
            P(("dp", "fsdp"), None),
            P("fsdp", None),
            P(),
            P(("dp", "fsdp"), None),
            P(("dp", "fsdp")),
        ),
        out_specs=(P(("dp", "fsdp")), P("fsdp", "dp")),
        check_vma=False,
    )
```

```python
import functools

import jax
import jax.numpy as jnp
from jax import lax
from jax.experimental import pallas as pl
from jax.experimental.pallas import tpu as pltpu
from jax.sharding import PartitionSpec as P

MESH = pl.DeviceIdType.MESH
F32 = jnp.float32
BF16 = jnp.bfloat16
NT = (((1,), (1,)), ((), ()))


def flip(index, mask):
    out = index
    bit = 1
    while bit <= mask:
        if mask & bit:
            out = out + bit * (1 - 2 * lax.rem(lax.div(index, bit), 2))
        bit *= 2
    return out


def count_copies(nd, nf):
    nz = nd // 4
    groups = nd // 2
    weights = (nf - 1) * (4 + 2 + 5 + 5 + 16)
    return weights + 16 * (nf - 1) + 1 + 4 * groups + (2 * nf - 1) * 2 * nz + nz + nz - 1


def kernel(
    nd,
    nf,
    seqs,
    context_hbm,
    residual_hbm,
    weight_hbm,
    gain_hbm,
    pattern_hbm,
    positive_ref,
    loss_ref,
    grad_ref,
    ctx,
    res,
    gain_ref,
    pattern_ref,
    wg,
    hid,
    invs,
    slopes,
    g_rows,
    ctx_t,
    ctx_all,
    note,
    notes,
    msg,
    pool,
    dhs,
    dh_all,
    y_send,
    y_recv,
    kept,
    z_send,
    z_recv,
    local_sem,
    send_sem,
    recv_sem,
):
    d = lax.axis_index("dp")
    f = lax.axis_index("fsdp")
    tokens, width = ctx.shape
    depth = wg.shape[1]
    nz = nd // 4
    bw = width // nd
    core = lax.rem(d, 2)
    y = lax.rem(lax.div(d, 2), 2)
    z = lax.div(d, 4)
    spot = lax.rem(d, 8)
    length = tokens // (2 * seqs)
    parts = 4
    rows_in = depth // 8
    wide = width // parts
    other = lambda k: lax.rem(f + k, nf)
    source = lambda k: lax.rem(f + nf - k, nf)
    others = range(1, nf)

    started = []

    def send(src, dst, dd, ff):
        slot = len(started)
        copy = pltpu.make_async_remote_copy(
            src_ref=src,
            dst_ref=dst,
            send_sem=send_sem.at[slot],
            recv_sem=recv_sem.at[slot],
            device_id=(dd, ff),
            device_id_type=MESH,
        )
        copy.start()
        started.append(copy)
        return copy

    def load(src, dst, slot):
        copy = pltpu.make_async_copy(src, dst, local_sem.at[slot])
        copy.start()
        return copy

    loads = [
        load(context_hbm, ctx, 0),
        load(weight_hbm, wg.at[f], 1),
        load(residual_hbm, res, 2),
        load(gain_hbm, gain_ref, 3),
        load(pattern_hbm, pattern_ref, 4),
    ]

    barrier = pltpu.get_barrier_semaphore()
    sibling = flip(d, 1)
    partners = [(lax.rem(d + 2 * s, nd), f) for s in range(1, nd // 2)] + [(sibling, f)]
    partners += [(d, other(k)) for k in others] + [(sibling, other(k)) for k in others]
    for partner in partners:
        pl.semaphore_signal(barrier, inc=1, device_id=partner, device_id_type=MESH)
    pl.semaphore_wait(barrier, len(partners))

    near_y, near_z, far = flip(spot, 2), flip(spot, 4), flip(spot, 6)

    def piece(place, h):
        row = (lax.rem(place, 2) * 4 + lax.div(place, 2)) * rows_in
        return (pl.ds(pl.multiple_of(row, rows_in), rows_in), slice(h * wide, (h + 1) * wide))

    def fetch(place, h):
        at = piece(place, h)
        return [send(weight_hbm.at[at], wg.at[(f, *at)], d, other(k)) for k in others]

    def pass_on(place, h, mask):
        at = piece(place, h)
        copies = []
        for k in others:
            ref = wg.at[(source(k), *at)]
            copies.append(send(ref, ref, flip(d, mask), f))
        return copies

    def arrive(copies):
        for copy in copies:
            copy.wait_recv()

    direct = {0: fetch(spot, 0)}

    groups = nd // 2
    slot_of_d = core * groups + lax.div(d, 2)
    core_slots = pl.ds(core * groups, groups)
    loads[4].wait()
    lanes = note.shape[1]
    lane_id = lax.broadcasted_iota(jnp.int32, (16, lanes), 1)
    row_id = lax.broadcasted_iota(jnp.int32, (16, lanes), 0)
    log_s = seqs.bit_length() - 1
    spread_lane = lax.broadcasted_iota(jnp.int32, (nd, lanes), 1) >> log_s
    spread = spread_lane == lax.broadcasted_iota(jnp.int32, (nd, lanes), 0)
    pattern = jnp.broadcast_to(pattern_ref[...].astype(F32), (16, nd)).astype(BF16)
    allowed_row = jnp.dot(
        pattern, jnp.where(spread, 1.0, 0.0).astype(BF16), preferred_element_type=F32
    )
    meta = jnp.where(row_id < seqs, allowed_row, 0.0)
    for s in range(seqs):
        hit = jnp.logical_and(row_id == seqs + s, lane_id == positive_ref[s] + d * seqs)
        meta = jnp.where(hit, 1.0, meta)
    note[...] = meta.astype(BF16)
    notes[slot_of_d] = note[...]
    near = [lax.rem(d + 2 * s, nd) for s in range(1, nd // 2)]
    note_copies = [send(note, notes.at[slot_of_d], there, f) for there in near]

    loads[0].wait()
    for part in range(nf):
        ctx_t[part] = ctx[:, part * depth : (part + 1) * depth].T
    direct[1] = fetch(spot, 1)
    ctx_all[core, f] = ctx_t[f]
    sibling_ctx = [send(ctx_all.at[core, f], ctx_all.at[core, f], sibling, f)]
    loads[1].wait()
    loads[2].wait()
    tile = 256

    def project(shard, first, start, count):
        def step(n, carry):
            cols = pl.ds(pl.multiple_of(n * tile, tile), tile)
            left = ctx[:, pl.ds(pl.multiple_of(shard * depth, 128), depth)]
            before = res[:, cols].astype(F32) if first else hid[:, cols]
            hid[:, cols] = before + jnp.dot(left, wg[shard, :, cols], preferred_element_type=F32)
            return carry

        lax.fori_loop(start // tile, (start + count) // tile, step, 0)

    arrive(direct[0])
    to_y, to_z, to_core, straight = {}, {}, {h: [] for h in range(parts)}, {}

    def spread_out(h):
        to_y[h] = pass_on(spot, h, 2)
        to_z[h] = pass_on(spot, h, 4)

    def to_sibling(h):
        rows = pl.ds(pl.multiple_of(core * 4 * rows_in, rows_in), 4 * rows_in)
        for k in others:
            ref = wg.at[source(k), rows, slice(h * wide, (h + 1) * wide)]
            to_core[h].append(send(ref, ref, sibling, f))

    def finish(h):
        arrive(to_core[h])
        for k in others:
            project(source(k), False, h * wide, wide)

    chunks = 1
    ctx_copies = {}

    def chunk(i):
        return slice(i * depth // chunks, (i + 1) * depth // chunks)

    def trickle(i):
        for k in others:
            src, dst = ctx_t.at[other(k), chunk(i)], ctx_all.at[core, f, chunk(i)]
            ctx_copies[i, k] = send(src, dst, d, other(k))

    def relay(i):
        for k in others:
            ctx_copies[i, k].wait_recv()
            ref = ctx_all.at[core, source(k), chunk(i)]
            sibling_ctx.append(send(ref, ref, sibling, f))

    spread_out(0)
    direct[2], straight[2] = fetch(spot, 2), fetch(far, 2)
    project(f, True, 0, width)
    arrive(direct[1])
    spread_out(1)
    direct[3], straight[3] = fetch(spot, 3), fetch(far, 3)
    arrive(to_z[0])
    across_y = pass_on(near_z, 0, 2)
    arrive(direct[2])
    spread_out(2)
    arrive(to_y[0])
    arrive(to_y[1])
    across_z = pass_on(near_y, 1, 4)
    arrive(across_y)
    to_sibling(0)
    arrive(direct[3])
    spread_out(3)
    trickle(0)
    arrive(to_z[1])
    arrive(across_z)
    to_sibling(1)
    finish(0)
    arrive(straight[2])
    arrive(to_y[2])
    arrive(to_z[2])
    to_sibling(2)
    finish(1)
    arrive(straight[3])
    arrive(to_y[3])
    arrive(to_z[3])
    to_sibling(3)
    finish(2)
    arrive(note_copies)
    note_pairs = [send(notes.at[core_slots], notes.at[core_slots], sibling, f)]
    finish(3)

    loads[3].wait()
    gain = gain_ref[...].astype(F32).reshape(1, width)
    pooled_rows = []
    for s in range(2 * seqs):
        rows = slice(s * length, (s + 1) * length)
        h_rows = hid[rows, :]
        inv = lax.rsqrt(jnp.mean(h_rows * h_rows, axis=1, keepdims=True) + 1e-05)
        invs[rows, :] = jnp.broadcast_to(inv, (length, invs.shape[1]))
        pooled_rows.append(jnp.sum(h_rows * inv, axis=0, keepdims=True))
    pooled = jnp.concatenate(pooled_rows, axis=0) * (gain / length)
    scale = lax.rsqrt(jnp.sum(pooled * pooled, axis=1, keepdims=True) + 1e-06)
    unit = pooled * scale
    per = 2 * seqs
    folds = 16 // per
    fold = width // folds
    folded = jnp.concatenate([unit[:, i * fold : (i + 1) * fold] for i in range(folds)], axis=0)
    msg[...] = folded.astype(BF16)
    pool_copies = [send(msg, pool.at[slot_of_d], there, f) for there in near]
    pool[slot_of_d] = msg[...]

    cols = nd * seqs
    total_rows = nd * 16
    log_p = per.bit_length() - 1
    flat = lax.broadcasted_iota(jnp.int32, (cols, total_rows), 1)
    col = lax.broadcasted_iota(jnp.int32, (cols, total_rows), 0)
    log_g = groups.bit_length() - 1
    device = (((flat >> 4) & (groups - 1)) << 1) + (flat >> (4 + log_g))
    owner = device == (col >> log_s)
    inner, slot_in = flat & (per - 1), col & (seqs - 1)
    pick_q = jnp.where(jnp.logical_and(owner, inner == slot_in), 1.0, 0.0).astype(BF16)
    pick_p = jnp.where(jnp.logical_and(owner, inner == slot_in + seqs), 1.0, 0.0).astype(BF16)
    row_fold = (lax.broadcasted_iota(jnp.int32, (total_rows, total_rows), 0) & 15) >> log_p
    col_fold = (lax.broadcasted_iota(jnp.int32, (total_rows, total_rows), 1) & 15) >> log_p
    same = jnp.where(row_fold == col_fold, 1.0, 0.0)
    lane_col = lax.broadcasted_iota(jnp.int32, (16, cols), 1) - d * seqs
    row_in = lax.broadcasted_iota(jnp.int32, (16, cols), 0) & (per - 1)
    hit_q = jnp.logical_and(lane_col == row_in, row_in < seqs)
    hit_p = jnp.logical_and(lane_col + seqs == row_in, row_in >= seqs)
    mine_q = jnp.where(hit_q, 1.0, 0.0).astype(BF16)
    mine_p = jnp.where(hit_p, 1.0, 0.0).astype(BF16)
    arrive(note_pairs)
    info = notes[...].reshape(total_rows, lanes)
    allowed = jnp.dot(pick_q, info, preferred_element_type=F32)[:, :cols]
    onehot = jnp.dot(pick_p, info, preferred_element_type=F32)[:, :cols]

    arrive(pool_copies)
    pool_pairs = [send(pool.at[core_slots], pool.at[core_slots], sibling, f)]
    relay(0)
    arrive(pool_pairs)

    def three(value):
        high = value.astype(BF16)
        rest = value - high.astype(F32)
        middle = rest.astype(BF16)
        return high, middle, (rest - middle.astype(F32)).astype(BF16)

    x = pool[...].reshape(total_rows, fold)
    gram = lax.dot_general(x, x, NT, preferred_element_type=F32) * same
    half = sum(jnp.dot(pick_q, part, preferred_element_type=F32) for part in three(gram))
    scores = 20.0 * sum(
        lax.dot_general(part, pick_p, NT, preferred_element_type=F32) for part in three(half)
    )
    weighted = allowed * jnp.exp(scores)
    total = jnp.sum(weighted, axis=1, keepdims=True)
    losses = jnp.log(total) - jnp.sum(onehot * scores, axis=1, keepdims=True)
    coeff = (weighted / total - onehot).astype(BF16)
    coeff_q = jnp.dot(mine_q, coeff, preferred_element_type=F32).astype(BF16)
    coeff_p = lax.dot_general(mine_p, coeff, NT, preferred_element_type=F32).astype(BF16)
    mix = jnp.dot(coeff_q, pick_p, preferred_element_type=F32)
    mix = mix + jnp.dot(coeff_p, pick_q, preferred_element_type=F32)
    mix = (mix * same[:16, :]).astype(BF16)
    d_fold = 20.0 * jnp.dot(mix, x, preferred_element_type=F32)
    d_embed = jnp.concatenate([d_fold[i * per : (i + 1) * per, :] for i in range(folds)], axis=1)
    d_pooled = (d_embed - unit * jnp.sum(unit * d_embed, axis=1, keepdims=True)) * scale
    d_gated = d_pooled * (gain / length)

    g_rows[0:per, :] = d_gated
    for s in range(per):
        rows = slice(s * length, (s + 1) * length)
        inv = invs[rows, 0:1]
        mean = jnp.mean(hid[rows, :] * d_gated[s : s + 1, :], axis=1, keepdims=True)
        slopes[rows, :] = jnp.broadcast_to(inv * inv * inv * mean, (length, slopes.shape[1]))

    def differentiate(block):
        at = pl.ds(pl.multiple_of(block * 4 * bw, 128), 4 * bw)
        for s in range(per):
            rows = slice(s * length, (s + 1) * length)
            inv, slope = invs[rows, 0:1], slopes[rows, 0:1]
            d_rows = inv * g_rows[s : s + 1, at] - hid[rows, at] * slope
            for j in range(4):
                dhs[j % 2, block, j // 2, rows, :] = d_rows[:, j * bw : (j + 1) * bw].astype(BF16)

    masks = list(range(nz - 1, -1, -1))
    peers = [(dc, k) for dc in range(2) for k in range(nf) if (dc, k) != (0, 0)]
    dh_copies = {}
    halves = [(masks[0], 1)]
    for ahead, mask in zip(masks[1:], masks):
        halves += [(ahead, 1), (mask, 0)]
    halves.append((masks[-1], 0))

    def share(mask, away):
        block, side = flip(z, mask), flip(y, away)
        for dc, k in peers:
            dh_copies[mask, away, dc, k] = send(
                dhs.at[flip(core, dc), block, side],
                dh_all.at[core, f, block, side],
                flip(d, dc),
                other(k),
            )

    for place, mask in enumerate(masks):
        differentiate(flip(z, mask))
        if place < 2:
            share(*halves[place])
    col_id = lax.broadcasted_iota(jnp.int32, (cols, 1), 0)
    for s in range(seqs):
        loss_ref[s] = jnp.sum(jnp.where(col_id == d * seqs + s, losses, 0.0))
    first_shared = len(started) - 2 * len(peers)
    for copy in started[:first_shared]:
        copy.wait_send()
    arrive(sibling_ctx)

    row_tile = min(256, depth)
    y_copies, z_copies = {}, {}

    def reduce_half(place):
        mask, away = halves[place]
        block, side = flip(z, mask), flip(y, away)
        for dc, k in peers:
            dh_copies[mask, away, dc, k].wait_recv()
        if place + 2 < len(halves):
            share(*halves[place + 2])

        def step(n, carry):
            at = pl.ds(pl.multiple_of(n * row_tile, row_tile), row_tile)
            total = jnp.dot(
                ctx_all[core, f, at, :], dhs[core, block, side], preferred_element_type=F32
            )
            for dc, k in peers:
                a, b = flip(core, dc), source(k)
                total += jnp.dot(
                    ctx_all[a, b, at, :], dh_all[a, b, block, side], preferred_element_type=F32
                )
            if away:
                y_send[mask, at, :] = total.astype(BF16)
            else:
                kept[mask, at, :] = total
            return carry

        lax.fori_loop(0, depth // row_tile, step, 0)
        if away:
            y_copies[mask] = send(y_send.at[mask], y_recv.at[mask], flip(d, 2), f)

    def forward_block(mask):
        y_copies[mask].wait_recv()
        summed = kept[mask] + y_recv[mask].astype(F32)
        bit = 1
        while bit < nz and not mask & bit:
            z_copies[mask | bit].wait_recv()
            summed = summed + z_recv[mask | bit].astype(F32)
            bit *= 2
        if mask:
            z_send[mask] = summed.astype(BF16)
            z_copies[mask] = send(z_send.at[mask], z_recv.at[mask], flip(d, 4 * bit), f)
        else:
            grad_ref[...] = summed

    for place, (mask, away) in enumerate(halves):
        reduce_half(place)
        if not away:
            forward_block(mask)
    for copy in started[first_shared:]:
        copy.wait_send()


def body(nd, nf, context, residual, weight, gain, pattern, positive):
    tokens, width = context.shape
    depth = weight.shape[0]
    seqs = positive.shape[0]
    nz = nd // 4
    bw = width // nd
    fold = width * 2 * seqs // 16
    lanes = 128
    vmem = pl.BlockSpec(memory_space=pltpu.VMEM)
    smem = pl.BlockSpec(memory_space=pltpu.SMEM)
    hbm = pl.BlockSpec(memory_space=pl.ANY)
    copies = count_copies(nd, nf)
    return pl.pallas_call(
        functools.partial(kernel, nd, nf, seqs),
        out_shape=(
            jax.ShapeDtypeStruct((seqs,), F32),
            jax.ShapeDtypeStruct((depth, bw), F32),
        ),
        in_specs=[hbm] * 5 + [smem],
        out_specs=(smem, vmem),
        scratch_shapes=[
            pltpu.VMEM((tokens, width), BF16),
            pltpu.VMEM((tokens, width), BF16),
            pltpu.VMEM((width,), BF16),
            pltpu.VMEM((1, nd), jnp.int32),
            pltpu.VMEM((nf, depth, width), BF16),
            pltpu.VMEM((tokens, width), F32),
            pltpu.VMEM((tokens, 128), F32),
            pltpu.VMEM((tokens, 128), F32),
            pltpu.VMEM((8, width), F32),
            pltpu.VMEM((nf, depth, tokens), BF16),
            pltpu.VMEM((2, nf, depth, tokens), BF16),
            pltpu.VMEM((16, lanes), BF16),
            pltpu.VMEM((nd, 16, lanes), BF16),
            pltpu.VMEM((16, fold), BF16),
            pltpu.VMEM((nd, 16, fold), BF16),
            pltpu.VMEM((2, nz, 2, tokens, bw), BF16),
            pltpu.VMEM((2, nf, nz, 2, tokens, bw), BF16),
            pltpu.VMEM((nz, depth, bw), BF16),
            pltpu.VMEM((nz, depth, bw), BF16),
            pltpu.VMEM((nz, depth, bw), F32),
            pltpu.VMEM((nz, depth, bw), BF16),
            pltpu.VMEM((nz, depth, bw), BF16),
            pltpu.SemaphoreType.DMA((5,)),
            pltpu.SemaphoreType.DMA((copies,)),
            pltpu.SemaphoreType.DMA((copies,)),
        ],
        compiler_params=pltpu.CompilerParams(
            collective_id=0, has_side_effects=True, vmem_limit_bytes=63 * 1024 * 1024
        ),
        cost_estimate=pl.CostEstimate(
            flops=8 * tokens * width * width, bytes_accessed=8 * depth * width, transcendentals=0
        ),
    )(context, residual, weight, gain, pattern, positive)


def solution(mesh):
    return jax.shard_map(
        functools.partial(body, mesh.shape["dp"], mesh.shape["fsdp"]),
        mesh=mesh,
        in_specs=(
            P(("dp", "fsdp"), None),
            P(("dp", "fsdp"), None),
            P("fsdp", None),
            P(),
            P(("dp", "fsdp"), None),
            P(("dp", "fsdp")),
        ),
        out_specs=(P(("dp", "fsdp")), P("fsdp", "dp")),
        check_vma=False,
    )
```

```python
import functools

import jax
import jax.numpy as jnp
from jax import lax
from jax.experimental import pallas as pl
from jax.experimental.pallas import tpu as pltpu
from jax.sharding import PartitionSpec as P

MESH = pl.DeviceIdType.MESH
F32 = jnp.float32
BF16 = jnp.bfloat16
NT = (((1,), (1,)), ((), ()))


def flip(index, mask):
    out = index
    bit = 1
    while bit <= mask:
        if mask & bit:
            out = out + bit * (1 - 2 * lax.rem(lax.div(index, bit), 2))
        bit *= 2
    return out


def count_copies(nd, nf):
    nz = nd // 4
    groups = nd // 2
    weights = (nf - 1) * (4 + 2 + 5 + 5 + 16)
    return weights + 16 * (nf - 1) + 1 + 4 * groups + (2 * nf - 1) * 2 * nz + nz + nz - 1


def kernel(
    nd,
    nf,
    seqs,
    context_hbm,
    residual_hbm,
    weight_hbm,
    gain_hbm,
    pattern_hbm,
    positive_ref,
    loss_ref,
    grad_ref,
    ctx,
    res,
    gain_ref,
    pattern_ref,
    wg,
    hid,
    invs,
    slopes,
    g_rows,
    ctx_t,
    ctx_all,
    note,
    notes,
    msg,
    pool,
    dhs,
    dh_all,
    y_send,
    y_recv,
    kept,
    z_send,
    z_recv,
    local_sem,
    send_sem,
    recv_sem,
):
    d = lax.axis_index("dp")
    f = lax.axis_index("fsdp")
    tokens, width = ctx.shape
    depth = wg.shape[1]
    nz = nd // 4
    bw = width // nd
    core = lax.rem(d, 2)
    y = lax.rem(lax.div(d, 2), 2)
    z = lax.div(d, 4)
    spot = lax.rem(d, 8)
    length = tokens // (2 * seqs)
    parts = 4
    rows_in = depth // 8
    wide = width // parts
    other = lambda k: lax.rem(f + k, nf)
    source = lambda k: lax.rem(f + nf - k, nf)
    others = range(1, nf)

    started = []

    def send(src, dst, dd, ff):
        slot = len(started)
        copy = pltpu.make_async_remote_copy(
            src_ref=src,
            dst_ref=dst,
            send_sem=send_sem.at[slot],
            recv_sem=recv_sem.at[slot],
            device_id=(dd, ff),
            device_id_type=MESH,
        )
        copy.start()
        started.append(copy)
        return copy

    def load(src, dst, slot):
        copy = pltpu.make_async_copy(src, dst, local_sem.at[slot])
        copy.start()
        return copy

    loads = [
        load(context_hbm, ctx, 0),
        load(weight_hbm, wg.at[f], 1),
        load(residual_hbm, res, 2),
        load(gain_hbm, gain_ref, 3),
        load(pattern_hbm, pattern_ref, 4),
    ]

    barrier = pltpu.get_barrier_semaphore()
    sibling = flip(d, 1)
    partners = [(lax.rem(d + 2 * s, nd), f) for s in range(1, nd // 2)] + [(sibling, f)]
    partners += [(d, other(k)) for k in others] + [(sibling, other(k)) for k in others]
    for partner in partners:
        pl.semaphore_signal(barrier, inc=1, device_id=partner, device_id_type=MESH)
    pl.semaphore_wait(barrier, len(partners))

    near_y, near_z, far = flip(spot, 2), flip(spot, 4), flip(spot, 6)

    def piece(place, h):
        row = (lax.rem(place, 2) * 4 + lax.div(place, 2)) * rows_in
        return (pl.ds(pl.multiple_of(row, rows_in), rows_in), slice(h * wide, (h + 1) * wide))

    def fetch(place, h):
        at = piece(place, h)
        return [send(weight_hbm.at[at], wg.at[(f, *at)], d, other(k)) for k in others]

    def pass_on(place, h, mask):
        at = piece(place, h)
        copies = []
        for k in others:
            ref = wg.at[(source(k), *at)]
            copies.append(send(ref, ref, flip(d, mask), f))
        return copies

    def arrive(copies):
        for copy in copies:
            copy.wait_recv()

    direct = {0: fetch(spot, 0)}

    groups = nd // 2
    slot_of_d = core * groups + lax.div(d, 2)
    core_slots = pl.ds(core * groups, groups)
    loads[4].wait()
    lanes = note.shape[1]
    lane_id = lax.broadcasted_iota(jnp.int32, (16, lanes), 1)
    row_id = lax.broadcasted_iota(jnp.int32, (16, lanes), 0)
    log_s = seqs.bit_length() - 1
    spread_lane = lax.broadcasted_iota(jnp.int32, (nd, lanes), 1) >> log_s
    spread = spread_lane == lax.broadcasted_iota(jnp.int32, (nd, lanes), 0)
    pattern = jnp.broadcast_to(pattern_ref[...].astype(F32), (16, nd)).astype(BF16)
    allowed_row = jnp.dot(
        pattern, jnp.where(spread, 1.0, 0.0).astype(BF16), preferred_element_type=F32
    )
    meta = jnp.where(row_id < seqs, allowed_row, 0.0)
    for s in range(seqs):
        hit = jnp.logical_and(row_id == seqs + s, lane_id == positive_ref[s] + d * seqs)
        meta = jnp.where(hit, 1.0, meta)
    note[...] = meta.astype(BF16)
    notes[slot_of_d] = note[...]
    near = [lax.rem(d + 2 * s, nd) for s in range(1, nd // 2)]
    note_copies = [send(note, notes.at[slot_of_d], there, f) for there in near]

    loads[0].wait()
    for part in range(nf):
        ctx_t[part] = ctx[:, part * depth : (part + 1) * depth].T
    direct[1] = fetch(spot, 1)
    ctx_all[core, f] = ctx_t[f]
    sibling_ctx = [send(ctx_all.at[core, f], ctx_all.at[core, f], sibling, f)]
    loads[1].wait()
    loads[2].wait()
    tile = 256

    def project(shard, first, start, count):
        def step(n, carry):
            cols = pl.ds(pl.multiple_of(n * tile, tile), tile)
            left = ctx[:, pl.ds(pl.multiple_of(shard * depth, 128), depth)]
            before = res[:, cols].astype(F32) if first else hid[:, cols]
            hid[:, cols] = before + jnp.dot(left, wg[shard, :, cols], preferred_element_type=F32)
            return carry

        lax.fori_loop(start // tile, (start + count) // tile, step, 0)

    arrive(direct[0])
    to_y, to_z, to_core, straight = {}, {}, {h: [] for h in range(parts)}, {}

    def spread_out(h):
        to_y[h] = pass_on(spot, h, 2)
        to_z[h] = pass_on(spot, h, 4)

    def to_sibling(h):
        rows = pl.ds(pl.multiple_of(core * 4 * rows_in, rows_in), 4 * rows_in)
        for k in others:
            ref = wg.at[source(k), rows, slice(h * wide, (h + 1) * wide)]
            to_core[h].append(send(ref, ref, sibling, f))

    def finish(h):
        arrive(to_core[h])
        for k in others:
            project(source(k), False, h * wide, wide)

    chunks = 1
    ctx_copies = {}

    def chunk(i):
        return slice(i * depth // chunks, (i + 1) * depth // chunks)

    def trickle(i):
        for k in others:
            src, dst = ctx_t.at[other(k), chunk(i)], ctx_all.at[core, f, chunk(i)]
            ctx_copies[i, k] = send(src, dst, d, other(k))

    def relay(i):
        for k in others:
            ctx_copies[i, k].wait_recv()
            ref = ctx_all.at[core, source(k), chunk(i)]
            sibling_ctx.append(send(ref, ref, sibling, f))

    spread_out(0)
    direct[2], straight[2] = fetch(spot, 2), fetch(far, 2)
    project(f, True, 0, width)
    arrive(direct[1])
    spread_out(1)
    direct[3], straight[3] = fetch(spot, 3), fetch(far, 3)
    arrive(to_z[0])
    across_y = pass_on(near_z, 0, 2)
    arrive(direct[2])
    spread_out(2)
    arrive(to_y[0])
    arrive(to_y[1])
    across_z = pass_on(near_y, 1, 4)
    arrive(across_y)
    to_sibling(0)
    arrive(direct[3])
    spread_out(3)
    trickle(0)
    arrive(to_z[1])
    arrive(across_z)
    to_sibling(1)
    finish(0)
    arrive(straight[2])
    arrive(to_y[2])
    arrive(to_z[2])
    to_sibling(2)
    finish(1)
    arrive(straight[3])
    arrive(to_y[3])
    arrive(to_z[3])
    to_sibling(3)
    finish(2)
    arrive(note_copies)
    note_pairs = [send(notes.at[core_slots], notes.at[core_slots], sibling, f)]
    finish(3)

    loads[3].wait()
    gain = gain_ref[...].astype(F32).reshape(1, width)
    pooled_rows = []
    for s in range(2 * seqs):
        rows = slice(s * length, (s + 1) * length)
        h_rows = hid[rows, :]
        inv = lax.rsqrt(jnp.mean(h_rows * h_rows, axis=1, keepdims=True) + 1e-05)
        invs[rows, :] = jnp.broadcast_to(inv, (length, invs.shape[1]))
        pooled_rows.append(jnp.sum(h_rows * inv, axis=0, keepdims=True))
    pooled = jnp.concatenate(pooled_rows, axis=0) * (gain / length)
    scale = lax.rsqrt(jnp.sum(pooled * pooled, axis=1, keepdims=True) + 1e-06)
    unit = pooled * scale
    per = 2 * seqs
    folds = 16 // per
    fold = width // folds
    folded = jnp.concatenate([unit[:, i * fold : (i + 1) * fold] for i in range(folds)], axis=0)
    msg[...] = folded.astype(BF16)
    pool_copies = [send(msg, pool.at[slot_of_d], there, f) for there in near]
    pool[slot_of_d] = msg[...]

    cols = nd * seqs
    total_rows = nd * 16
    log_p = per.bit_length() - 1
    flat = lax.broadcasted_iota(jnp.int32, (cols, total_rows), 1)
    col = lax.broadcasted_iota(jnp.int32, (cols, total_rows), 0)
    log_g = groups.bit_length() - 1
    device = (((flat >> 4) & (groups - 1)) << 1) + (flat >> (4 + log_g))
    owner = device == (col >> log_s)
    inner, slot_in = flat & (per - 1), col & (seqs - 1)
    pick_q = jnp.where(jnp.logical_and(owner, inner == slot_in), 1.0, 0.0).astype(BF16)
    pick_p = jnp.where(jnp.logical_and(owner, inner == slot_in + seqs), 1.0, 0.0).astype(BF16)
    row_fold = (lax.broadcasted_iota(jnp.int32, (total_rows, total_rows), 0) & 15) >> log_p
    col_fold = (lax.broadcasted_iota(jnp.int32, (total_rows, total_rows), 1) & 15) >> log_p
    same = jnp.where(row_fold == col_fold, 1.0, 0.0)
    lane_col = lax.broadcasted_iota(jnp.int32, (16, cols), 1) - d * seqs
    row_in = lax.broadcasted_iota(jnp.int32, (16, cols), 0) & (per - 1)
    hit_q = jnp.logical_and(lane_col == row_in, row_in < seqs)
    hit_p = jnp.logical_and(lane_col + seqs == row_in, row_in >= seqs)
    mine_q = jnp.where(hit_q, 1.0, 0.0).astype(BF16)
    mine_p = jnp.where(hit_p, 1.0, 0.0).astype(BF16)
    arrive(note_pairs)
    info = notes[...].reshape(total_rows, lanes)
    allowed = jnp.dot(pick_q, info, preferred_element_type=F32)[:, :cols]
    onehot = jnp.dot(pick_p, info, preferred_element_type=F32)[:, :cols]

    arrive(pool_copies)
    pool_pairs = [send(pool.at[core_slots], pool.at[core_slots], sibling, f)]
    relay(0)
    arrive(pool_pairs)

    def three(value):
        high = value.astype(BF16)
        rest = value - high.astype(F32)
        middle = rest.astype(BF16)
        return high, middle, (rest - middle.astype(F32)).astype(BF16)

    x = pool[...].reshape(total_rows, fold)
    gram = lax.dot_general(x, x, NT, preferred_element_type=F32) * same
    half = sum(jnp.dot(pick_q, part, preferred_element_type=F32) for part in three(gram))
    scores = 20.0 * sum(
        lax.dot_general(part, pick_p, NT, preferred_element_type=F32) for part in three(half)
    )
    weighted = allowed * jnp.exp(scores)
    total = jnp.sum(weighted, axis=1, keepdims=True)
    losses = jnp.log(total) - jnp.sum(onehot * scores, axis=1, keepdims=True)
    coeff = (weighted / total - onehot).astype(BF16)
    coeff_q = jnp.dot(mine_q, coeff, preferred_element_type=F32).astype(BF16)
    coeff_p = lax.dot_general(mine_p, coeff, NT, preferred_element_type=F32).astype(BF16)
    mix = jnp.dot(coeff_q, pick_p, preferred_element_type=F32)
    mix = mix + jnp.dot(coeff_p, pick_q, preferred_element_type=F32)
    mix = (mix * same[:16, :]).astype(BF16)
    d_fold = 20.0 * jnp.dot(mix, x, preferred_element_type=F32)
    d_embed = jnp.concatenate([d_fold[i * per : (i + 1) * per, :] for i in range(folds)], axis=1)
    d_pooled = (d_embed - unit * jnp.sum(unit * d_embed, axis=1, keepdims=True)) * scale
    d_gated = d_pooled * (gain / length)

    g_rows[0:per, :] = d_gated
    for s in range(per):
        rows = slice(s * length, (s + 1) * length)
        inv = invs[rows, 0:1]
        mean = jnp.mean(hid[rows, :] * d_gated[s : s + 1, :], axis=1, keepdims=True)
        slopes[rows, :] = jnp.broadcast_to(inv * inv * inv * mean, (length, slopes.shape[1]))

    def differentiate(block):
        at = pl.ds(pl.multiple_of(block * 4 * bw, 128), 4 * bw)
        for s in range(per):
            rows = slice(s * length, (s + 1) * length)
            inv, slope = invs[rows, 0:1], slopes[rows, 0:1]
            d_rows = inv * g_rows[s : s + 1, at] - hid[rows, at] * slope
            for j in range(4):
                dhs[j % 2, block, j // 2, rows, :] = d_rows[:, j * bw : (j + 1) * bw].astype(BF16)

    masks = list(range(nz - 1, -1, -1))
    peers = [(dc, k) for dc in range(2) for k in range(nf) if (dc, k) != (0, 0)]
    dh_copies = {}
    halves = [(masks[0], 1)]
    for ahead, mask in zip(masks[1:], masks):
        halves += [(ahead, 1), (mask, 0)]
    halves.append((masks[-1], 0))

    def share(mask, away):
        block, side = flip(z, mask), flip(y, away)
        for dc, k in peers:
            dh_copies[mask, away, dc, k] = send(
                dhs.at[flip(core, dc), block, side],
                dh_all.at[core, f, block, side],
                flip(d, dc),
                other(k),
            )

    for place, mask in enumerate(masks):
        differentiate(flip(z, mask))
        if place < 2:
            share(*halves[place])
        if place == 1:
            share(*halves[2])
    col_id = lax.broadcasted_iota(jnp.int32, (cols, 1), 0)
    for s in range(seqs):
        loss_ref[s] = jnp.sum(jnp.where(col_id == d * seqs + s, losses, 0.0))
    first_shared = len(started) - 3 * len(peers)
    for copy in started[:first_shared]:
        copy.wait_send()
    arrive(sibling_ctx)

    row_tile = min(256, depth)
    y_copies, z_copies = {}, {}

    def reduce_half(place):
        mask, away = halves[place]
        block, side = flip(z, mask), flip(y, away)
        for dc, k in peers:
            dh_copies[mask, away, dc, k].wait_recv()
        if place + 3 < len(halves):
            share(*halves[place + 3])

        def step(n, carry):
            at = pl.ds(pl.multiple_of(n * row_tile, row_tile), row_tile)
            total = jnp.dot(
                ctx_all[core, f, at, :], dhs[core, block, side], preferred_element_type=F32
            )
            for dc, k in peers:
                a, b = flip(core, dc), source(k)
                total += jnp.dot(
                    ctx_all[a, b, at, :], dh_all[a, b, block, side], preferred_element_type=F32
                )
            if away:
                y_send[mask, at, :] = total.astype(BF16)
            else:
                kept[mask, at, :] = total
            return carry

        lax.fori_loop(0, depth // row_tile, step, 0)
        if away:
            y_copies[mask] = send(y_send.at[mask], y_recv.at[mask], flip(d, 2), f)

    def forward_block(mask):
        y_copies[mask].wait_recv()
        summed = kept[mask] + y_recv[mask].astype(F32)
        bit = 1
        while bit < nz and not mask & bit:
            z_copies[mask | bit].wait_recv()
            summed = summed + z_recv[mask | bit].astype(F32)
            bit *= 2
        if mask:
            z_send[mask] = summed.astype(BF16)
            z_copies[mask] = send(z_send.at[mask], z_recv.at[mask], flip(d, 4 * bit), f)
        else:
            grad_ref[...] = summed

    for place, (mask, away) in enumerate(halves):
        reduce_half(place)
        if not away:
            forward_block(mask)
    for copy in started[first_shared:]:
        copy.wait_send()


def body(nd, nf, context, residual, weight, gain, pattern, positive):
    tokens, width = context.shape
    depth = weight.shape[0]
    seqs = positive.shape[0]
    nz = nd // 4
    bw = width // nd
    fold = width * 2 * seqs // 16
    lanes = 128
    vmem = pl.BlockSpec(memory_space=pltpu.VMEM)
    smem = pl.BlockSpec(memory_space=pltpu.SMEM)
    hbm = pl.BlockSpec(memory_space=pl.ANY)
    copies = count_copies(nd, nf)
    return pl.pallas_call(
        functools.partial(kernel, nd, nf, seqs),
        out_shape=(
            jax.ShapeDtypeStruct((seqs,), F32),
            jax.ShapeDtypeStruct((depth, bw), F32),
        ),
        in_specs=[hbm] * 5 + [smem],
        out_specs=(smem, vmem),
        scratch_shapes=[
            pltpu.VMEM((tokens, width), BF16),
            pltpu.VMEM((tokens, width), BF16),
            pltpu.VMEM((width,), BF16),
            pltpu.VMEM((1, nd), jnp.int32),
            pltpu.VMEM((nf, depth, width), BF16),
            pltpu.VMEM((tokens, width), F32),
            pltpu.VMEM((tokens, 128), F32),
            pltpu.VMEM((tokens, 128), F32),
            pltpu.VMEM((8, width), F32),
            pltpu.VMEM((nf, depth, tokens), BF16),
            pltpu.VMEM((2, nf, depth, tokens), BF16),
            pltpu.VMEM((16, lanes), BF16),
            pltpu.VMEM((nd, 16, lanes), BF16),
            pltpu.VMEM((16, fold), BF16),
            pltpu.VMEM((nd, 16, fold), BF16),
            pltpu.VMEM((2, nz, 2, tokens, bw), BF16),
            pltpu.VMEM((2, nf, nz, 2, tokens, bw), BF16),
            pltpu.VMEM((nz, depth, bw), BF16),
            pltpu.VMEM((nz, depth, bw), BF16),
            pltpu.VMEM((nz, depth, bw), F32),
            pltpu.VMEM((nz, depth, bw), BF16),
            pltpu.VMEM((nz, depth, bw), BF16),
            pltpu.SemaphoreType.DMA((5,)),
            pltpu.SemaphoreType.DMA((copies,)),
            pltpu.SemaphoreType.DMA((copies,)),
        ],
        compiler_params=pltpu.CompilerParams(
            collective_id=0, has_side_effects=True, vmem_limit_bytes=63 * 1024 * 1024
        ),
        cost_estimate=pl.CostEstimate(
            flops=8 * tokens * width * width, bytes_accessed=8 * depth * width, transcendentals=0
        ),
    )(context, residual, weight, gain, pattern, positive)


def solution(mesh):
    return jax.shard_map(
        functools.partial(body, mesh.shape["dp"], mesh.shape["fsdp"]),
        mesh=mesh,
        in_specs=(
            P(("dp", "fsdp"), None),
            P(("dp", "fsdp"), None),
            P("fsdp", None),
            P(),
            P(("dp", "fsdp"), None),
            P(("dp", "fsdp")),
        ),
        out_specs=(P(("dp", "fsdp")), P("fsdp", "dp")),
        check_vma=False,
    )
```
